256 devices in a mesh: dp: 4 (over z_lo, core), ctx: 64 (over y, x, z_hi).
Axes of the slice: x: 4, y: 4, z: 8 (z_hi: 4, z_lo: 2; z = z_hi * 2 + z_lo), core: 2. Of those that a mesh axis runs over, the one named last changes fastest.
Arguments:
- projections: bfloat16 [4, 3, 2048, 8192], P('dp', None, None, 'ctx'), may hold values from -6 to 6
- short_filter: float32 [3, 2048, 3], replicated, may hold values from -3.5 to 3.5
- long_filter: float32 [2048, 8192], P(None, 'ctx'), may hold values from -0.0625 to 0.0625
- skip_gain: float32 [2048], replicated, may hold values from -4 to 4
- cotangent: bfloat16 [4, 2048, 8192], P('dp', None, 'ctx'), may hold values from -6 to 6
Outputs:
- layer_out: bfloat16 [4, 2048, 8192], P('dp', None, 'ctx')
- proj_grad: bfloat16 [4, 3, 2048, 8192], P('dp', None, None, 'ctx')
- filter_grad: float32 [2048, 8192], P('dp', 'ctx')
The draws below stay inside these ranges and needn't reach their ends.
All inputs are finite; a program needn't handle non-finite values.
Results may differ from the reference program's by a relative error of at most 0.0049.
Values may be sent and summed in bfloat16 or wider, within the bound.
A program may use at most 128 MiB of HBM per device.

```python
import math
import jax
import jax.numpy as jnp
from jax import lax

C = 2048
LENGTH = 8192
SEQS = 4


def block_scale(key, dims, split, least, high):
    loudness, own = 1.0, jax.random.fold_in(key, 6)
    for axis_at, parts in split:
        draws = jnp.exp(jax.random.uniform(jax.random.fold_in(own, axis_at), (parts,), jnp.float32, least / len(split), high / len(split)))
        loudness = loudness * jnp.repeat(draws, dims[axis_at] // parts).reshape([-1 if axis == axis_at else 1 for axis in range(len(dims))])
    return loudness


def normal_values(rng, extent, scale, reach, pieces=(), dtype=jnp.bfloat16):
    entries = scale * jax.random.normal(rng, extent, jnp.float32)
    if pieces:
        entries = entries * block_scale(rng, extent, pieces, -0.22, 0.18)
    return jnp.clip(entries, -reach, reach).astype(dtype)


def setup_inputs(seed: int = 0) -> dict:
    key_of = jax.random.split(jax.random.key(seed), 6)
    projections = normal_values(key_of[0], (SEQS, 3, C, LENGTH), 1.0, 6.0, ((0, 4), (3, 64)))
    short_filter = normal_values(key_of[1], (3, C, 3), 3 ** -0.5, 3.5, (), jnp.float32)
    long_filter = normal_values(key_of[2], (C, LENGTH), LENGTH ** -0.5, 0.0625, ((1, 64),), jnp.float32)
    skip_gain = normal_values(key_of[3], (C,), 1.0, 4.0, (), jnp.float32)
    cotangent = normal_values(key_of[4], (SEQS, C, LENGTH), 1.0, 6.0, ((0, 4), (2, 64)))
    return {"projections": projections, "short_filter": short_filter, "long_filter": long_filter, "skip_gain": skip_gain, "cotangent": cotangent}


def delayed(values, steps):
    padded = jnp.pad(values, ((0, 0), (0, 0), (steps, 0)))
    return padded[:, :, :LENGTH]

def advanced(values, steps):
    padded = jnp.pad(values, ((0, 0), (0, 0), (0, steps)))
    return padded[:, :, steps:]

def reference(projections, short_filter, long_filter, skip_gain, cotangent):
    fft_size = 2 * LENGTH
    filter_spec = jnp.fft.rfft(long_filter, n=fft_size, axis=-1)
    tap_zero = short_filter[:, :, 0:1]
    tap_one = short_filter[:, :, 1:2]
    tap_two = short_filter[:, :, 2:3]
    skip_col = skip_gain[:, None]
    scale = 1.0 / math.sqrt(SEQS * LENGTH)
    outs_list = []
    grads_list = []
    filter_total = jnp.zeros((C, LENGTH), jnp.float32)
    for index in range(SEQS):
        inputs = projections[index].astype(jnp.float32)
        act = tap_zero * inputs + tap_one * delayed(inputs, 1) + tap_two * delayed(inputs, 2)
        first = act[0]
        second = act[1]
        value = act[2]
        gate = lax.optimization_barrier((first * value).astype(jnp.bfloat16)).astype(jnp.float32)
        gate_spec = jnp.fft.rfft(gate, n=fft_size, axis=-1)
        conv = jnp.fft.irfft(filter_spec * gate_spec, n=fft_size, axis=-1)[:, :LENGTH]
        mixed = conv + skip_col * gate
        outs_list.append((second * mixed).astype(jnp.bfloat16))
        upstream = cotangent[index].astype(jnp.float32)
        grad = lax.optimization_barrier((upstream * second).astype(jnp.bfloat16)).astype(jnp.float32)
        grad_spec = jnp.fft.rfft(grad, n=fft_size, axis=-1)
        corr = jnp.fft.irfft(jnp.conj(filter_spec) * grad_spec, n=fft_size, axis=-1)[:, :LENGTH]
        filter_total = filter_total + jnp.fft.irfft(jnp.conj(gate_spec) * grad_spec, n=fft_size, axis=-1)[:, :LENGTH]
        gate_grad = corr + skip_col * grad
        act_grad = jnp.stack([gate_grad * value, upstream * mixed, gate_grad * first])
        proj_back = tap_zero * act_grad + tap_one * advanced(act_grad, 1) + tap_two * advanced(act_grad, 2)
        grads_list.append(proj_back.astype(jnp.bfloat16))
    return (jnp.stack(outs_list), jnp.stack(grads_list), filter_total * scale)
```

```python
import functools
import math

import jax
import jax.numpy as jnp
import ml_dtypes
import numpy as np
from jax import lax
from jax.experimental import pallas as pl
from jax.experimental.pallas import tpu as pltpu
from jax.sharding import PartitionSpec as P

DP = 4
CTX = 64
CHANNELS = 2048
LANES = 128
BLOCK = CHANNELS // DP
OWN = BLOCK // CTX
ROWS = OWN * CTX
POINTS = 2 * CTX * LANES
MESH = pl.DeviceIdType.MESH
F32 = jnp.float32
BF16 = jnp.bfloat16


def halves(table):
    high = table.astype(ml_dtypes.bfloat16)
    low = (table - high.astype(np.float64)).astype(ml_dtypes.bfloat16)
    return high, low


def tables():
    freq = np.arange(CTX) + 0.5
    block_angle = 2 * np.pi * np.outer(freq, np.arange(CTX)) / LANES
    first = np.concatenate([np.cos(block_angle), -np.sin(block_angle)], 0)
    first_hi, first_lo = halves(first)
    enter = np.concatenate([first_hi, first_lo], 1)
    enter_wide = np.concatenate([first_hi, first_lo, first_hi], 1)
    last = np.concatenate([np.cos(block_angle.T), -np.sin(block_angle.T)], 1) * (2.0 / POINTS)
    last_hi, last_lo = halves(last)
    leave = np.concatenate([last_hi, last_lo], 1)
    inner = np.arange(LANES)
    inner_angle = 2 * np.pi * (np.outer(inner, inner) % LANES) / LANES
    c, s = np.cos(inner_angle), np.sin(inner_angle)
    spread_hi, spread_lo = halves(np.concatenate([np.concatenate([c, -s], 1), np.concatenate([s, c], 1)], 0))
    gather_hi, gather_lo = halves(np.concatenate([np.concatenate([c, s], 1), np.concatenate([-s, c], 1)], 0))
    twist = 2 * np.pi * np.outer(freq, inner) / POINTS
    turn = np.stack([np.cos(twist), np.sin(twist)]).astype(np.float32)
    widen = np.zeros((48, 10 * LANES), ml_dtypes.bfloat16)
    for part in range(3):
        for v in range(10):
            widen[16 * part + v, LANES * v : LANES * (v + 1)] = 1
    pick = np.zeros((2, 3, 8, LANES), ml_dtypes.bfloat16)
    place = np.zeros((2, 24, 3 * LANES), ml_dtypes.bfloat16)
    for m in range(3):
        for e in range(2):
            pick[0, m, 2 * m + e, LANES - 2 + e] = 1
            pick[1, m, 2 * m + e, e] = 1
            for part in range(3):
                place[0, 8 * part + 2 * m + e, LANES * m + e] = 1
                place[1, 8 * part + 2 * m + e, LANES * m + LANES - 2 + e] = 1
    return (enter, enter_wide, leave, spread_hi, spread_lo, gather_hi, gather_lo, turn, widen, pick, place)


def dot(a, b):
    return lax.dot_general(a, b, (((1,), (0,)), ((), ())), preferred_element_type=F32)


def dot_tn(a, b):
    return lax.dot_general(a, b, (((0,), (0,)), ((), ())), preferred_element_type=F32)


def dot_nt(a, b):
    return lax.dot_general(a, b, (((1,), (1,)), ((), ())), preferred_element_type=F32)


def split2(value):
    high = value.astype(BF16)
    return high, (value - high.astype(F32)).astype(BF16)


def split3(value):
    high = value.astype(BF16)
    rest = value - high.astype(F32)
    mid = rest.astype(BF16)
    return jnp.concatenate([high, mid, (rest - mid.astype(F32)).astype(BF16)], 0)


def loop(count, body, unroll=1):
    def step(i, carry):
        body(i)
        return carry

    lax.fori_loop(0, count, step, 0, unroll=unroll)


def kernel(
    proj, cot, filt, taps,
    enter, enter_wide, leave, spread_hi, spread_lo, gather_hi, gather_lo, turn, widen, pick, place,
    out_y, out_p, out_f,
    wide, acts, edge, sbuf, rbuf, csbuf, crbuf, frecv, fspec, total, work, zhi, zlo, spec, gsend, grecv,
    hx_send, hx_recv, hg_send, hg_recv,
    fwd_send, fwd_recv, back_send, back_recv, hg_ssem, hg_rsem, misc,
):
    d = lax.axis_index("dp")
    j = lax.axis_index("ctx")
    jy, jx, jz = j // 16, (j // 4) % 4, j % 4

    def peer(n):
        dy, dx, dz = n // 16, (n // 4) % 4, n % 4
        return (((jy + dy) % 4) * 4 + (jx + dx) % 4) * 4 + (jz + dz) % 4

    def others(i, act):
        def body(n):
            pl.when(jnp.logical_or(n > 0, i > 0))(lambda: act(peer(n)))

        loop(CTX, body)

    def wait_bytes(ref, sem):
        pltpu.make_async_copy(ref, ref, sem).wait()

    @pl.when(j == 0)
    def _():
        hx_recv[...] = jnp.zeros_like(hx_recv)

    @pl.when(j == CTX - 1)
    def _():
        hg_recv[...] = jnp.zeros_like(hg_recv)

    barrier = pltpu.get_barrier_semaphore()

    def greet(i):
        other = (d + i) % DP
        others(i, lambda t: pl.semaphore_signal(barrier, inc=1, device_id=(other, t), device_id_type=MESH))

    loop(DP, greet)

    def prepare(b):
        cols = pl.ds(pl.multiple_of(b * BLOCK, BLOCK), BLOCK)
        wide[cols, :] = dot_tn(split3(taps[:, cols]), widen[...])
        picked = dot_nt(pick[0, 0], proj[0, cols, :])
        for m in range(1, 3):
            picked += dot_nt(pick[0, m], proj[m, cols, :])
        tap = taps[:, cols]
        rows = []
        for m in range(3):
            before, last = picked[2 * m : 2 * m + 1], picked[2 * m + 1 : 2 * m + 2]
            one, two = tap[3 * m + 1 : 3 * m + 2], tap[3 * m + 2 : 3 * m + 3]
            rows += [one * last + two * before, two * last]
        rows.append(jnp.zeros((2, BLOCK), F32))
        hx_send[b] = jnp.concatenate(rows, 0)

    loop(DP, prepare)
    pl.semaphore_wait(barrier, DP * CTX - 1)

    def halo_copy():
        return pltpu.make_async_remote_copy(
            src_ref=hx_send, dst_ref=hx_recv, send_sem=misc.at[0], recv_sem=misc.at[1],
            device_id=(d, jnp.minimum(j + 1, CTX - 1)), device_id_type=MESH)

    pl.when(j < CTX - 1)(lambda: halo_copy().start())

    def send_filter(t):
        pltpu.make_async_remote_copy(
            src_ref=filt.at[pl.ds(pl.multiple_of(d * BLOCK + t * OWN, OWN), OWN), :],
            dst_ref=frecv.at[pl.ds(pl.multiple_of(j * OWN, OWN), OWN), :],
            send_sem=misc.at[2], recv_sem=misc.at[3], device_id=(d, t), device_id_type=MESH).start()

    others(0, send_filter)
    frecv[pl.ds(pl.multiple_of(j * OWN, OWN), OWN), :] = filt[pl.ds(pl.multiple_of(d * BLOCK + j * OWN, OWN), OWN), :]
    pl.when(j > 0)(lambda: wait_bytes(hx_recv, misc.at[1]))

    lane = lax.broadcasted_iota(jnp.int32, (2 * OWN, LANES), 1)

    def lanes_of(v):
        return slice(LANES * v, LANES * (v + 1))

    def gates(i):
        b = (d + i) % DP
        edge[...] = dot_tn(split3(hx_recv[b]), place[0])

        def group(g):
            here = pl.ds(pl.multiple_of(g * 2 * OWN, 2 * OWN), 2 * OWN)
            rows = pl.ds(pl.multiple_of(b * BLOCK + g * 2 * OWN, 2 * OWN), 2 * OWN)
            act = []
            for m in range(3):
                x = proj[m, rows, :].astype(F32)
                one = jnp.where(lane >= 1, pltpu.roll(x, 1, 1), 0.0)
                two = jnp.where(lane >= 2, pltpu.roll(x, 2, 1), 0.0)
                value = (
                    wide[rows, lanes_of(3 * m)] * x
                    + wide[rows, lanes_of(3 * m + 1)] * one
                    + wide[rows, lanes_of(3 * m + 2)] * two
                    + edge[here, lanes_of(m)]
                )
                acts[m, rows, :] = value
                act.append(value)
            gate = act[0] * act[2]
            grad = cot[rows, :].astype(F32) * act[1]
            for e in range(2):
                part = slice(OWN * e, OWN * (e + 1))
                sbuf[i, 2 * g + e] = jnp.concatenate([gate[part], grad[part]], 0).astype(BF16)

        loop(CTX // 2, group, unroll=2)

        def send(t):
            pltpu.make_async_remote_copy(
                src_ref=sbuf.at[i, t], dst_ref=rbuf.at[i, j], send_sem=fwd_send.at[i], recv_sem=fwd_recv.at[i],
                device_id=(b, t), device_id_type=MESH).start()

        others(i, send)

    loop(DP, gates)
    rbuf[0, j] = sbuf[0, j]

    def turned(real, imag, way):
        c, s = turn[0], turn[1]
        if way > 0:
            return real * c - imag * s, real * s + imag * c
        return real * c + imag * s, imag * c - real * s

    def put(rows, real, imag):
        for part, value in ((slice(0, LANES), real), (slice(LANES, 2 * LANES), imag)):
            high, low = split2(value)
            zhi[rows, part] = high
            zlo[rows, part] = low

    def across(count, table_hi, table_lo, into):
        def body(k):
            rows = pl.ds(pl.multiple_of(k * 512, 512), 512)
            into[rows, :] = (
                dot(zhi[rows, :], table_hi[...]) + dot(zlo[rows, :], table_hi[...]) + dot(zhi[rows, :], table_lo[...])
            )

        loop(count // 512, body)

    def rows_of(c):
        return pl.ds(pl.multiple_of(c * CTX, CTX), CTX)

    def enter_pair(product, row_left, row_right):
        for row, side in ((row_left, slice(0, LANES)), (row_right, slice(LANES, 2 * LANES))):
            put(rows_of(row), *turned(product[:CTX, side], product[CTX:, side], -1))

    def leave_pair(row_left, row_right):
        left = turned(spec[rows_of(row_left), :LANES], spec[rows_of(row_left), LANES:], 1)
        right = turned(spec[rows_of(row_right), :LANES], spec[rows_of(row_right), LANES:], 1)
        both = jnp.concatenate([jnp.concatenate([a, b], 1) for a, b in zip(left, right)], 0)
        high, low = split2(both)
        return dot(leave[...], jnp.concatenate([high, high], 0)) + dot(leave[:, :LANES], low)

    wait_bytes(frecv.at[pl.ds(0, ROWS - OWN), :], misc.at[3])

    def filter_enter(c):
        pair = jnp.concatenate(
            [frecv[pl.ds(c, CTX, stride=OWN), :], frecv[pl.ds(c + OWN // 2, CTX, stride=OWN), :]], 1
        )
        high, low = split2(pair)
        enter_pair(dot(enter_wide[...], jnp.concatenate([high, high, low], 0)), c, c + OWN // 2)

    loop(OWN // 2, filter_enter)
    across(ROWS, spread_hi, spread_lo, fspec)
    total[...] = jnp.zeros_like(total)

    def convolve(i):
        @pl.when(i == 0)
        def _():
            wait_bytes(rbuf.at[0, pl.ds(0, CTX - 1)], fwd_recv.at[0])

        @pl.when(i > 0)
        def _():
            wait_bytes(rbuf.at[i], fwd_recv.at[i])

        def unpack(p):
            work[pl.ds(pl.multiple_of(p * 2 * OWN, 2 * OWN), 2 * OWN), :] = rbuf[i, p].astype(F32)

        loop(CTX, unpack, unroll=8)

        def one_enter(c):
            pair = jnp.concatenate(
                [work[pl.ds(c, CTX, stride=2 * OWN), :], work[pl.ds(c + OWN, CTX, stride=2 * OWN), :]], 1
            ).astype(BF16)
            enter_pair(dot(enter[...], jnp.concatenate([pair, pair], 0)), c, c + OWN)

        loop(OWN, one_enter, unroll=2)
        across(2 * ROWS, spread_hi, spread_lo, spec)

        def products(c):
            fr, fi = fspec[rows_of(c), :LANES], fspec[rows_of(c), LANES:]
            gr, gi = spec[rows_of(c), :LANES], spec[rows_of(c), LANES:]
            dr, di = spec[rows_of(c + OWN), :LANES], spec[rows_of(c + OWN), LANES:]
            put(rows_of(c), fr * gr - fi * gi, fr * gi + fi * gr)
            put(rows_of(c + OWN), fr * dr + fi * di, fr * di - fi * dr)
            total[rows_of(c), :LANES] += gr * dr + gi * di
            total[rows_of(c), LANES:] += gr * di - gi * dr

        loop(OWN, products)
        across(2 * ROWS, gather_hi, gather_lo, spec)

        def one_leave(c):
            result = leave_pair(c, c + OWN)
            work[pl.ds(c, CTX, stride=2 * OWN), :] = result[:, :LANES]
            work[pl.ds(c + OWN, CTX, stride=2 * OWN), :] = result[:, LANES:]

        loop(OWN, one_leave, unroll=2)

        def pack(p):
            csbuf[i, p] = work[pl.ds(pl.multiple_of(p * 2 * OWN, 2 * OWN), 2 * OWN), :].astype(BF16)

        loop(CTX, pack, unroll=8)
        home = (d + DP - i) % DP

        def send(t):
            pltpu.make_async_remote_copy(
                src_ref=csbuf.at[i, t], dst_ref=crbuf.at[i, j], send_sem=back_send.at[i], recv_sem=back_recv.at[i],
                device_id=(home, t), device_id_type=MESH).start()

        others(i, send)

    loop(DP, convolve)
    crbuf[0, j] = csbuf[0, j]

    def total_rows(c):
        put(rows_of(c), total[rows_of(c), :LANES], total[rows_of(c), LANES:])

    loop(OWN, total_rows)
    across(ROWS, gather_hi, gather_lo, spec)
    scale = 1.0 / math.sqrt(DP * CTX * LANES)

    def filter_leave(c):
        result = leave_pair(c, c + OWN // 2) * scale
        gsend[pl.ds(c, CTX, stride=OWN), :] = result[:, :LANES]
        gsend[pl.ds(c + OWN // 2, CTX, stride=OWN), :] = result[:, LANES:]

    loop(OWN // 2, filter_leave)

    def send_grad(t):
        pltpu.make_async_remote_copy(
            src_ref=gsend.at[pl.ds(pl.multiple_of(t * OWN, OWN), OWN), :],
            dst_ref=grecv.at[pl.ds(pl.multiple_of(j * OWN, OWN), OWN), :],
            send_sem=misc.at[4], recv_sem=misc.at[5], device_id=(d, t), device_id_type=MESH).start()

    others(0, send_grad)
    mine = pl.ds(pl.multiple_of(j * OWN, OWN), OWN)
    grecv[mine, :] = gsend[mine, :]

    def grad_halo(i):
        b = (d + i) % DP
        return pltpu.make_async_remote_copy(
            src_ref=hg_send.at[b], dst_ref=hg_recv.at[b], send_sem=hg_ssem.at[i], recv_sem=hg_rsem.at[i],
            device_id=(d, jnp.maximum(j - 1, 0)), device_id_type=MESH)

    def outputs(i):
        b = (d + i) % DP

        @pl.when(i == 0)
        def _():
            wait_bytes(crbuf.at[0, pl.ds(0, CTX - 1)], back_recv.at[0])

        @pl.when(i > 0)
        def _():
            wait_bytes(crbuf.at[i], back_recv.at[i])

        def group(g):
            rows = pl.ds(pl.multiple_of(b * BLOCK + g * 2 * OWN, 2 * OWN), 2 * OWN)
            own = [sbuf[i, 2 * g + e].astype(F32) for e in range(2)]
            back = [crbuf[i, 2 * g + e].astype(F32) for e in range(2)]
            gate = jnp.concatenate([own[0][:OWN], own[1][:OWN]], 0)
            grad = jnp.concatenate([own[0][OWN:], own[1][OWN:]], 0)
            conv = jnp.concatenate([back[0][:OWN], back[1][:OWN]], 0)
            corr = jnp.concatenate([back[0][OWN:], back[1][OWN:]], 0)
            gain = wide[rows, lanes_of(9)]
            mixed = conv + gain * gate
            gate_grad = corr + gain * grad
            first, second, value = acts[0, rows, :], acts[1, rows, :], acts[2, rows, :]
            out_y[rows, :] = (second * mixed).astype(BF16)
            acts[0, rows, :] = gate_grad * value
            acts[1, rows, :] = cot[rows, :].astype(F32) * mixed
            acts[2, rows, :] = gate_grad * first

        loop(CTX // 2, group, unroll=2)
        cols = pl.ds(pl.multiple_of(b * BLOCK, BLOCK), BLOCK)
        picked = dot_nt(pick[1, 0], acts[0, cols, :].astype(BF16))
        for m in range(1, 3):
            picked += dot_nt(pick[1, m], acts[m, cols, :].astype(BF16))
        tap = taps[:, cols]
        rows = []
        for m in range(3):
            near, far = picked[2 * m : 2 * m + 1], picked[2 * m + 1 : 2 * m + 2]
            one, two = tap[3 * m + 1 : 3 * m + 2], tap[3 * m + 2 : 3 * m + 3]
            rows += [two * near, one * near + two * far]
        rows.append(jnp.zeros((2, BLOCK), F32))
        hg_send[b] = jnp.concatenate(rows, 0)
        pl.when(j > 0)(lambda: grad_halo(i).start())

    def finish(i):
        b = (d + i) % DP
        pl.when(j < CTX - 1)(lambda: grad_halo(i).wait_recv())
        edge[...] = dot_tn(split3(hg_recv[b]), place[1])

        def group(g):
            here = pl.ds(pl.multiple_of(g * 2 * OWN, 2 * OWN), 2 * OWN)
            rows = pl.ds(pl.multiple_of(b * BLOCK + g * 2 * OWN, 2 * OWN), 2 * OWN)
            for m in range(3):
                x = acts[m, rows, :]
                one = jnp.where(lane < LANES - 1, pltpu.roll(x, LANES - 1, 1), 0.0)
                two = jnp.where(lane < LANES - 2, pltpu.roll(x, LANES - 2, 1), 0.0)
                value = (
                    wide[rows, lanes_of(3 * m)] * x
                    + wide[rows, lanes_of(3 * m + 1)] * one
                    + wide[rows, lanes_of(3 * m + 2)] * two
                    + edge[here, lanes_of(m)]
                )
                out_p[m, rows, :] = value.astype(BF16)

        loop(CTX // 2, group, unroll=2)

    def tail(i):
        pl.when(i < DP)(lambda: outputs(i))
        pl.when(i > 0)(lambda: finish(i - 1))

    loop(DP + 1, tail)

    wait_bytes(grecv.at[pl.ds(0, ROWS - OWN), :], misc.at[5])
    out_f[...] = grecv[...]

    pl.when(j < CTX - 1)(lambda: halo_copy().wait_send())
    wait_bytes(frecv.at[pl.ds(0, ROWS - OWN), :], misc.at[2])
    wait_bytes(gsend.at[pl.ds(0, ROWS - OWN), :], misc.at[4])
    for i in range(DP):
        count = CTX - 1 if i == 0 else CTX
        wait_bytes(sbuf.at[i, pl.ds(0, count)], fwd_send.at[i])
        wait_bytes(csbuf.at[i, pl.ds(0, count)], back_send.at[i])
        pl.when(j > 0)(lambda i=i: grad_halo(i).wait_send())


def shards(projections, short_filter, long_filter, skip_gain, cotangent):
    taps = jnp.concatenate(
        [short_filter.transpose(0, 2, 1).reshape(9, CHANNELS), skip_gain[None], jnp.zeros((6, CHANNELS), F32)], 0
    )
    constants = tables()
    vmem = pl.BlockSpec(memory_space=pltpu.VMEM)
    dma = pltpu.SemaphoreType.DMA
    layer_out, proj_grad, filter_grad = pl.pallas_call(
        kernel,
        out_shape=(
            jax.ShapeDtypeStruct((CHANNELS, LANES), BF16),
            jax.ShapeDtypeStruct((3, CHANNELS, LANES), BF16),
            jax.ShapeDtypeStruct((ROWS, LANES), F32),
        ),
        in_specs=[vmem] * (4 + len(constants)),
        out_specs=(vmem, vmem, vmem),
        scratch_shapes=[
            pltpu.VMEM((CHANNELS, 10 * LANES), F32),
            pltpu.VMEM((3, CHANNELS, LANES), F32),
            pltpu.VMEM((BLOCK, 3 * LANES), F32),
            pltpu.VMEM((DP, CTX, 2 * OWN, LANES), BF16),
            pltpu.VMEM((DP, CTX, 2 * OWN, LANES), BF16),
            pltpu.VMEM((DP, CTX, 2 * OWN, LANES), BF16),
            pltpu.VMEM((DP, CTX, 2 * OWN, LANES), BF16),
            pltpu.VMEM((ROWS, LANES), F32),
            pltpu.VMEM((ROWS, 2 * LANES), F32),
            pltpu.VMEM((ROWS, 2 * LANES), F32),
            pltpu.VMEM((2 * ROWS, LANES), F32),
            pltpu.VMEM((2 * ROWS, 2 * LANES), BF16),
            pltpu.VMEM((2 * ROWS, 2 * LANES), BF16),
            pltpu.VMEM((2 * ROWS, 2 * LANES), F32),
            pltpu.VMEM((ROWS, LANES), F32),
            pltpu.VMEM((ROWS, LANES), F32),
            pltpu.VMEM((DP, 8, BLOCK), F32),
            pltpu.VMEM((DP, 8, BLOCK), F32),
            pltpu.VMEM((DP, 8, BLOCK), F32),
            pltpu.VMEM((DP, 8, BLOCK), F32),
            dma((DP,)), dma((DP,)), dma((DP,)), dma((DP,)), dma((DP,)), dma((DP,)), dma((6,)),
        ],
        compiler_params=pltpu.CompilerParams(
            collective_id=0, has_side_effects=True, vmem_limit_bytes=60 * 1024 * 1024
        ),
    )(projections[0], cotangent[0], long_filter, taps, *constants)
    return layer_out[None], proj_grad[None], filter_grad


def solution(mesh):
    placed = (P("dp", None, None, "ctx"), P(), P(None, "ctx"), P(), P("dp", None, "ctx"))
    return jax.shard_map(
        shards,
        mesh=mesh,
        in_specs=placed,
        out_specs=(P("dp", None, "ctx"), P("dp", None, None, "ctx"), P("dp", "ctx")),
        check_vma=False,
    )
```

```python
import functools
import math

import jax
import jax.numpy as jnp
import ml_dtypes
import numpy as np
from jax import lax
from jax.experimental import pallas as pl
from jax.experimental.pallas import tpu as pltpu
from jax.sharding import PartitionSpec as P

DP = 4
CTX = 64
CHANNELS = 2048
LANES = 128
BLOCK = CHANNELS // DP
OWN = BLOCK // CTX
ROWS = OWN * CTX
POINTS = 2 * CTX * LANES
MESH = pl.DeviceIdType.MESH
F32 = jnp.float32
BF16 = jnp.bfloat16


def halves(table):
    high = table.astype(ml_dtypes.bfloat16)
    low = (table - high.astype(np.float64)).astype(ml_dtypes.bfloat16)
    return high, low


def tables():
    freq = np.arange(CTX) + 0.5
    block_angle = 2 * np.pi * np.outer(freq, np.arange(CTX)) / LANES
    first = np.concatenate([np.cos(block_angle), -np.sin(block_angle)], 0)
    first_hi, first_lo = halves(first)
    enter = np.concatenate([first_hi, first_lo], 1)
    last = np.concatenate([np.cos(block_angle.T), -np.sin(block_angle.T)], 1) * (2.0 / POINTS)
    last_hi, last_lo = halves(last)
    leave = np.concatenate([last_hi, last_lo], 1)
    inner = np.arange(LANES)
    inner_angle = 2 * np.pi * (np.outer(inner, inner) % LANES) / LANES
    c, s = np.cos(inner_angle), np.sin(inner_angle)
    spread_hi, spread_lo = halves(np.concatenate([np.concatenate([c, -s], 1), np.concatenate([s, c], 1)], 0))
    gather_hi, gather_lo = halves(np.concatenate([np.concatenate([c, s], 1), np.concatenate([-s, c], 1)], 0))
    twist = 2 * np.pi * np.outer(freq, inner) / POINTS
    turn = np.stack([np.cos(twist), np.sin(twist)]).astype(np.float32)
    widen = np.zeros((48, 10 * LANES), ml_dtypes.bfloat16)
    for part in range(3):
        for v in range(10):
            widen[16 * part + v, LANES * v : LANES * (v + 1)] = 1
    pick = np.zeros((2, 3, 8, LANES), ml_dtypes.bfloat16)
    place = np.zeros((2, 24, 3 * LANES), ml_dtypes.bfloat16)
    for m in range(3):
        for e in range(2):
            pick[0, m, 2 * m + e, LANES - 2 + e] = 1
            pick[1, m, 2 * m + e, e] = 1
            for part in range(3):
                place[0, 8 * part + 2 * m + e, LANES * m + e] = 1
                place[1, 8 * part + 2 * m + e, LANES * m + LANES - 2 + e] = 1
    return (enter, leave, spread_hi, spread_lo, gather_hi, gather_lo, turn, widen, pick, place)


def dot(a, b):
    return lax.dot_general(a, b, (((1,), (0,)), ((), ())), preferred_element_type=F32)


def dot_tn(a, b):
    return lax.dot_general(a, b, (((0,), (0,)), ((), ())), preferred_element_type=F32)


def dot_nt(a, b):
    return lax.dot_general(a, b, (((1,), (1,)), ((), ())), preferred_element_type=F32)


def split2(value):
    high = value.astype(BF16)
    return high, (value - high.astype(F32)).astype(BF16)


def split3(value):
    high = value.astype(BF16)
    rest = value - high.astype(F32)
    mid = rest.astype(BF16)
    return jnp.concatenate([high, mid, (rest - mid.astype(F32)).astype(BF16)], 0)


def loop(count, body, unroll=1):
    def step(i, carry):
        body(i)
        return carry

    lax.fori_loop(0, count, step, 0, unroll=unroll)


def kernel(
    proj_hbm, cot_hbm, filt_hbm, taps_hbm, gain_hbm, *refs,
):
    constants_hbm, refs = refs[:10], refs[10:]
    out_y, out_p, out_f = refs[:3]
    constants, refs = refs[3:13], refs[13:]
    enter, leave, spread_hi, spread_lo, gather_hi, gather_lo, turn, widen, pick, place = constants
    (
        proj, cot, filt, taps3, gains, taps,
        wide, acts, edge, sbuf, rbuf, csbuf, crbuf, fsend, frecv, fspec, total, work, zhi, zlo, spec, gsend, grecv,
        hx_send, hx_recv, hg_send, hg_recv,
        fwd_send, fwd_recv, back_send, back_recv, hg_ssem, hg_rsem, misc, in_sem, const_sem,
    ) = refs
    d = lax.axis_index("dp")
    j = lax.axis_index("ctx")
    jy, jx, jz = j // 16, (j // 4) % 4, j % 4

    near = [((jx + n // 4) % 4) * 4 + (jz + n % 4) % 4 for n in range(16)]

    def others(i, act):
        def body(dy):
            plane = ((jy + dy) % 4) * 16
            pl.when(jnp.logical_or(dy > 0, i > 0))(lambda: act(plane + near[0]))
            for n in range(1, 16):
                act(plane + near[n])

        loop(4, body)

    def wait_bytes(ref, sem):
        pltpu.make_async_copy(ref, ref, sem).wait()

    rows_d = pl.ds(pl.multiple_of(d * BLOCK, BLOCK), BLOCK)
    loads = [
        pltpu.make_async_copy(source, target, in_sem.at[n])
        for n, (source, target) in enumerate((
            (proj_hbm, proj), (taps_hbm, taps3), (gain_hbm, gains), (filt_hbm.at[rows_d, :], filt), (cot_hbm, cot)))
    ]
    loads += [
        pltpu.make_async_copy(source, target, const_sem.at[n])
        for n, (source, target) in reversed(list(enumerate(zip(constants_hbm, constants))))
    ]
    for load in loads:
        load.start()

    @pl.when(j == 0)
    def _():
        hx_recv[...] = jnp.zeros_like(hx_recv)

    @pl.when(j == CTX - 1)
    def _():
        hg_recv[...] = jnp.zeros_like(hg_recv)

    barrier = pltpu.get_barrier_semaphore()

    def greet(i):
        other = (d + i) % DP
        others(i, lambda t: pl.semaphore_signal(barrier, inc=1, device_id=(other, t), device_id_type=MESH))

    loop(DP, greet)

    for load in loads[:3] + loads[5:8]:
        load.wait()
    taps[...] = jnp.zeros_like(taps)
    for m in range(3):
        taps[3 * m : 3 * m + 3, :] = taps3[m]
    taps[9:10, :] = gains[...]

    def prepare(b):
        cols = pl.ds(pl.multiple_of(b * BLOCK, BLOCK), BLOCK)
        picked = dot_nt(pick[0, 0], proj[0, cols, :])
        for m in range(1, 3):
            picked += dot_nt(pick[0, m], proj[m, cols, :])
        tap = taps[:, cols]
        rows = []
        for m in range(3):
            before, last = picked[2 * m : 2 * m + 1], picked[2 * m + 1 : 2 * m + 2]
            one, two = tap[3 * m + 1 : 3 * m + 2], tap[3 * m + 2 : 3 * m + 3]
            rows += [one * last + two * before, two * last]
        rows.append(jnp.zeros((2, BLOCK), F32))
        hx_send[b] = jnp.concatenate(rows, 0)

    loop(DP, prepare)
    loads[3].wait()

    def narrow(t):
        fsend[t] = filt[pl.ds(pl.multiple_of(t * OWN, OWN), OWN), :].astype(BF16)

    loop(CTX, narrow, unroll=8)
    pl.semaphore_wait(barrier, DP * CTX - 1)

    def halo_copy():
        return pltpu.make_async_remote_copy(
            src_ref=hx_send, dst_ref=hx_recv, send_sem=misc.at[0], recv_sem=misc.at[1],
            device_id=(d, jnp.minimum(j + 1, CTX - 1)), device_id_type=MESH)

    pl.when(j < CTX - 1)(lambda: halo_copy().start())

    def send_filter(t):
        pltpu.make_async_remote_copy(
            src_ref=fsend.at[t], dst_ref=frecv.at[j],
            send_sem=misc.at[2], recv_sem=misc.at[3], device_id=(d, t), device_id_type=MESH).start()

    others(0, send_filter)
    frecv[j] = fsend[j]
    loads[4].wait()

    def spread_taps(b):
        cols = pl.ds(pl.multiple_of(b * BLOCK, BLOCK), BLOCK)
        wide[cols, :] = dot_tn(split3(taps[:, cols]), widen[...])

    spread_taps(d)
    pl.when(j > 0)(lambda: wait_bytes(hx_recv, misc.at[1]))

    lane = lax.broadcasted_iota(jnp.int32, (2 * OWN, LANES), 1)

    def lanes_of(v):
        return slice(LANES * v, LANES * (v + 1))

    def gates(i):
        b = (d + i) % DP
        pl.when(i > 0)(lambda: spread_taps(b))
        edge[...] = dot_tn(split3(hx_recv[b]), place[0])

        def group(g):
            here = pl.ds(pl.multiple_of(g * 2 * OWN, 2 * OWN), 2 * OWN)
            rows = pl.ds(pl.multiple_of(b * BLOCK + g * 2 * OWN, 2 * OWN), 2 * OWN)
            act = []
            for m in range(3):
                x = proj[m, rows, :].astype(F32)
                one = jnp.where(lane >= 1, pltpu.roll(x, 1, 1), 0.0)
                two = jnp.where(lane >= 2, pltpu.roll(x, 2, 1), 0.0)
                value = (
                    wide[rows, lanes_of(3 * m)] * x
                    + wide[rows, lanes_of(3 * m + 1)] * one
                    + wide[rows, lanes_of(3 * m + 2)] * two
                    + edge[here, lanes_of(m)]
                )
                acts[m, rows, :] = value
                act.append(value)
            gate = act[0] * act[2]
            grad = cot[rows, :].astype(F32) * act[1]
            for e in range(2):
                part = slice(OWN * e, OWN * (e + 1))
                sbuf[i, 2 * g + e] = jnp.concatenate([gate[part], grad[part]], 0).astype(BF16)

        loop(CTX // 2, group, unroll=2)

        def send(t):
            pltpu.make_async_remote_copy(
                src_ref=sbuf.at[i, t], dst_ref=rbuf.at[i, j], send_sem=fwd_send.at[i], recv_sem=fwd_recv.at[i],
                device_id=(b, t), device_id_type=MESH).start()

        others(i, send)

    loop(DP, gates)
    rbuf[0, j] = sbuf[0, j]

    def turned(real, imag, way):
        c, s = turn[0], turn[1]
        if way > 0:
            return real * c - imag * s, real * s + imag * c
        return real * c + imag * s, imag * c - real * s

    def put(rows, real, imag):
        for part, value in ((slice(0, LANES), real), (slice(LANES, 2 * LANES), imag)):
            high, low = split2(value)
            zhi[rows, part] = high
            zlo[rows, part] = low

    def across(count, table_hi, table_lo, into):
        def body(k):
            rows = pl.ds(pl.multiple_of(k * 512, 512), 512)
            into[rows, :] = (
                dot(zhi[rows, :], table_hi[...]) + dot(zlo[rows, :], table_hi[...]) + dot(zhi[rows, :], table_lo[...])
            )

        loop(count // 512, body)

    def rows_of(c):
        return pl.ds(pl.multiple_of(c * CTX, CTX), CTX)

    def enter_pair(product, row_left, row_right):
        for row, side in ((row_left, slice(0, LANES)), (row_right, slice(LANES, 2 * LANES))):
            put(rows_of(row), *turned(product[:CTX, side], product[CTX:, side], -1))

    def leave_pair(row_left, row_right):
        left = turned(spec[rows_of(row_left), :LANES], spec[rows_of(row_left), LANES:], 1)
        right = turned(spec[rows_of(row_right), :LANES], spec[rows_of(row_right), LANES:], 1)
        both = jnp.concatenate([jnp.concatenate([a, b], 1) for a, b in zip(left, right)], 0)
        high, low = split2(both)
        return dot(leave[...], jnp.concatenate([high, high], 0)) + dot(leave[:, :LANES], low)

    for load in loads[8:]:
        load.wait()
    wait_bytes(frecv.at[pl.ds(0, CTX - 1)], misc.at[3])

    def filter_unpack(p):
        work[pl.ds(pl.multiple_of(p * OWN, OWN), OWN), :] = frecv[p].astype(F32)

    loop(CTX, filter_unpack, unroll=8)

    def filter_enter(c):
        pair = jnp.concatenate(
            [work[pl.ds(c, CTX, stride=OWN), :], work[pl.ds(c + OWN // 2, CTX, stride=OWN), :]], 1
        ).astype(BF16)
        enter_pair(dot(enter[...], jnp.concatenate([pair, pair], 0)), c, c + OWN // 2)

    loop(OWN // 2, filter_enter)
    across(ROWS, spread_hi, spread_lo, fspec)
    total[...] = jnp.zeros_like(total)

    def convolve(i):
        @pl.when(i == 0)
        def _():
            wait_bytes(rbuf.at[0, pl.ds(0, CTX - 1)], fwd_recv.at[0])

        @pl.when(i > 0)
        def _():
            wait_bytes(rbuf.at[i], fwd_recv.at[i])

        def unpack(p):
            work[pl.ds(pl.multiple_of(p * 2 * OWN, 2 * OWN), 2 * OWN), :] = rbuf[i, p].astype(F32)

        loop(CTX, unpack, unroll=8)

        def one_enter(c):
            pair = jnp.concatenate(
                [work[pl.ds(c, CTX, stride=2 * OWN), :], work[pl.ds(c + OWN, CTX, stride=2 * OWN), :]], 1
            ).astype(BF16)
            enter_pair(dot(enter[...], jnp.concatenate([pair, pair], 0)), c, c + OWN)

        loop(OWN, one_enter, unroll=2)
        across(2 * ROWS, spread_hi, spread_lo, spec)

        def products(c):
            fr, fi = fspec[rows_of(c), :LANES], fspec[rows_of(c), LANES:]
            gr, gi = spec[rows_of(c), :LANES], spec[rows_of(c), LANES:]
            dr, di = spec[rows_of(c + OWN), :LANES], spec[rows_of(c + OWN), LANES:]
            put(rows_of(c), fr * gr - fi * gi, fr * gi + fi * gr)
            put(rows_of(c + OWN), fr * dr + fi * di, fr * di - fi * dr)
            total[rows_of(c), :LANES] += gr * dr + gi * di
            total[rows_of(c), LANES:] += gr * di - gi * dr

        loop(OWN, products)
        across(2 * ROWS, gather_hi, gather_lo, spec)

        def one_leave(c):
            result = leave_pair(c, c + OWN)
            work[pl.ds(c, CTX, stride=2 * OWN), :] = result[:, :LANES]
            work[pl.ds(c + OWN, CTX, stride=2 * OWN), :] = result[:, LANES:]

        loop(OWN, one_leave, unroll=2)

        def pack(p):
            csbuf[i, p] = work[pl.ds(pl.multiple_of(p * 2 * OWN, 2 * OWN), 2 * OWN), :].astype(BF16)

        loop(CTX, pack, unroll=8)
        home = (d + DP - i) % DP

        def send(t):
            pltpu.make_async_remote_copy(
                src_ref=csbuf.at[i, t], dst_ref=crbuf.at[i, j], send_sem=back_send.at[i], recv_sem=back_recv.at[i],
                device_id=(home, t), device_id_type=MESH).start()

        others(i, send)

    loop(DP, convolve)
    crbuf[0, j] = csbuf[0, j]

    def total_rows(c):
        put(rows_of(c), total[rows_of(c), :LANES], total[rows_of(c), LANES:])

    loop(OWN, total_rows)
    across(ROWS, gather_hi, gather_lo, spec)
    scale = 1.0 / math.sqrt(DP * CTX * LANES)

    def filter_leave(c):
        result = leave_pair(c, c + OWN // 2) * scale
        work[pl.ds(c, CTX, stride=OWN), :] = result[:, :LANES]
        work[pl.ds(c + OWN // 2, CTX, stride=OWN), :] = result[:, LANES:]

    loop(OWN // 2, filter_leave)

    def filter_pack(p):
        gsend[p] = work[pl.ds(pl.multiple_of(p * OWN, OWN), OWN), :].astype(BF16)

    loop(CTX, filter_pack, unroll=8)

    def send_grad(t):
        pltpu.make_async_remote_copy(
            src_ref=gsend.at[t], dst_ref=grecv.at[j],
            send_sem=misc.at[4], recv_sem=misc.at[5], device_id=(d, t), device_id_type=MESH).start()

    others(0, send_grad)
    grecv[j] = gsend[j]

    def grad_halo(i):
        b = (d + i) % DP
        return pltpu.make_async_remote_copy(
            src_ref=hg_send.at[b], dst_ref=hg_recv.at[b], send_sem=hg_ssem.at[i], recv_sem=hg_rsem.at[i],
            device_id=(d, jnp.maximum(j - 1, 0)), device_id_type=MESH)

    def outputs(i):
        b = (d + i) % DP

        @pl.when(i == 0)
        def _():
            wait_bytes(crbuf.at[0, pl.ds(0, CTX - 1)], back_recv.at[0])

        @pl.when(i > 0)
        def _():
            wait_bytes(crbuf.at[i], back_recv.at[i])

        def group(g):
            rows = pl.ds(pl.multiple_of(b * BLOCK + g * 2 * OWN, 2 * OWN), 2 * OWN)
            own = [sbuf[i, 2 * g + e].astype(F32) for e in range(2)]
            back = [crbuf[i, 2 * g + e].astype(F32) for e in range(2)]
            gate = jnp.concatenate([own[0][:OWN], own[1][:OWN]], 0)
            grad = jnp.concatenate([own[0][OWN:], own[1][OWN:]], 0)
            conv = jnp.concatenate([back[0][:OWN], back[1][:OWN]], 0)
            corr = jnp.concatenate([back[0][OWN:], back[1][OWN:]], 0)
            gain = wide[rows, lanes_of(9)]
            mixed = conv + gain * gate
            gate_grad = corr + gain * grad
            first, second, value = acts[0, rows, :], acts[1, rows, :], acts[2, rows, :]
            out_y[rows, :] = (second * mixed).astype(BF16)
            acts[0, rows, :] = gate_grad * value
            acts[1, rows, :] = cot[rows, :].astype(F32) * mixed
            acts[2, rows, :] = gate_grad * first

        loop(CTX // 2, group, unroll=2)
        cols = pl.ds(pl.multiple_of(b * BLOCK, BLOCK), BLOCK)
        picked = dot_nt(pick[1, 0], acts[0, cols, :].astype(BF16))
        for m in range(1, 3):
            picked += dot_nt(pick[1, m], acts[m, cols, :].astype(BF16))
        tap = taps[:, cols]
        rows = []
        for m in range(3):
            near, far = picked[2 * m : 2 * m + 1], picked[2 * m + 1 : 2 * m + 2]
            one, two = tap[3 * m + 1 : 3 * m + 2], tap[3 * m + 2 : 3 * m + 3]
            rows += [two * near, one * near + two * far]
        rows.append(jnp.zeros((2, BLOCK), F32))
        hg_send[b] = jnp.concatenate(rows, 0)
        pl.when(j > 0)(lambda: grad_halo(i).start())

    def finish(i):
        b = (d + i) % DP
        pl.when(j < CTX - 1)(lambda: grad_halo(i).wait_recv())
        edge[...] = dot_tn(split3(hg_recv[b]), place[1])

        def group(g):
            here = pl.ds(pl.multiple_of(g * 2 * OWN, 2 * OWN), 2 * OWN)
            rows = pl.ds(pl.multiple_of(b * BLOCK + g * 2 * OWN, 2 * OWN), 2 * OWN)
            for m in range(3):
                x = acts[m, rows, :]
                one = jnp.where(lane < LANES - 1, pltpu.roll(x, LANES - 1, 1), 0.0)
                two = jnp.where(lane < LANES - 2, pltpu.roll(x, LANES - 2, 1), 0.0)
                value = (
                    wide[rows, lanes_of(3 * m)] * x
                    + wide[rows, lanes_of(3 * m + 1)] * one
                    + wide[rows, lanes_of(3 * m + 2)] * two
                    + edge[here, lanes_of(m)]
                )
                out_p[m, rows, :] = value.astype(BF16)

        loop(CTX // 2, group, unroll=2)

    def tail(i):
        pl.when(i < DP)(lambda: outputs(i))
        pl.when(i > 0)(lambda: finish(i - 1))

    loop(DP + 1, tail)

    wait_bytes(grecv.at[pl.ds(0, CTX - 1)], misc.at[5])

    def filter_out(p):
        out_f[pl.ds(pl.multiple_of(p * OWN, OWN), OWN), :] = grecv[p].astype(F32)

    loop(CTX, filter_out, unroll=8)

    pl.when(j < CTX - 1)(lambda: halo_copy().wait_send())
    wait_bytes(fsend.at[pl.ds(0, CTX - 1)], misc.at[2])
    wait_bytes(gsend.at[pl.ds(0, CTX - 1)], misc.at[4])
    for i in range(DP):
        count = CTX - 1 if i == 0 else CTX
        wait_bytes(sbuf.at[i, pl.ds(0, count)], fwd_send.at[i])
        wait_bytes(csbuf.at[i, pl.ds(0, count)], back_send.at[i])
        pl.when(j > 0)(lambda i=i: grad_halo(i).wait_send())


def hand_over(*refs):
    count = len(refs) // 2
    sem = refs[-1]
    copies = [
        pltpu.make_async_copy(refs[n], refs[count + n], sem.at[n]) for n in range(count)
    ]
    for copy in copies:
        copy.start()
    for copy in copies:
        copy.wait()


def shards(projections, short_filter, long_filter, skip_gain, cotangent):
    constants = tables()
    near = pl.BlockSpec(memory_space=pltpu.VMEM)
    hbm = pl.BlockSpec(memory_space=pltpu.HBM)
    dma = pltpu.SemaphoreType.DMA
    vmem = pltpu.VMEM
    outs = (
        jax.ShapeDtypeStruct((CHANNELS, LANES), BF16),
        jax.ShapeDtypeStruct((3, CHANNELS, LANES), BF16),
        jax.ShapeDtypeStruct((ROWS, LANES), F32),
    )
    operands = (
        projections[0], cotangent[0], long_filter, short_filter.transpose(0, 2, 1), skip_gain[None], *constants
    )
    results = pl.pallas_call(
        kernel,
        out_shape=tuple(vmem(out.shape, out.dtype) for out in outs),
        in_specs=[hbm] * (5 + len(constants)),
        out_specs=(near,) * 3,
        scratch_shapes=[vmem(table.shape, jnp.dtype(table.dtype)) for table in constants]
        + [
            vmem((3, CHANNELS, LANES), BF16),
            vmem((CHANNELS, LANES), BF16),
            vmem((BLOCK, LANES), F32),
            vmem((3, 3, CHANNELS), F32),
            vmem((1, CHANNELS), F32),
            vmem((16, CHANNELS), F32),
            vmem((CHANNELS, 10 * LANES), F32),
            vmem((3, CHANNELS, LANES), F32),
            vmem((BLOCK, 3 * LANES), F32),
            vmem((DP, CTX, 2 * OWN, LANES), BF16),
            vmem((DP, CTX, 2 * OWN, LANES), BF16),
            vmem((DP, CTX, 2 * OWN, LANES), BF16),
            vmem((DP, CTX, 2 * OWN, LANES), BF16),
            vmem((CTX, OWN, LANES), BF16),
            vmem((CTX, OWN, LANES), BF16),
            vmem((ROWS, 2 * LANES), F32),
            vmem((ROWS, 2 * LANES), F32),
            vmem((2 * ROWS, LANES), F32),
            vmem((2 * ROWS, 2 * LANES), BF16),
            vmem((2 * ROWS, 2 * LANES), BF16),
            vmem((2 * ROWS, 2 * LANES), F32),
            vmem((CTX, OWN, LANES), BF16),
            vmem((CTX, OWN, LANES), BF16),
            vmem((DP, 8, BLOCK), F32),
            vmem((DP, 8, BLOCK), F32),
            vmem((DP, 8, BLOCK), F32),
            vmem((DP, 8, BLOCK), F32),
            dma((DP,)), dma((DP,)), dma((DP,)), dma((DP,)), dma((DP,)), dma((DP,)), dma((6,)),
            dma((5,)), dma((len(constants),)),
        ],
        compiler_params=pltpu.CompilerParams(
            collective_id=0, has_side_effects=True, vmem_limit_bytes=48 * 1024 * 1024
        ),
    )(*[pltpu.with_memory_space_constraint(operand, pltpu.HBM) for operand in operands])
    layer_out, proj_grad, filter_grad = pl.pallas_call(
        hand_over,
        out_shape=outs,
        in_specs=[near] * 3,
        out_specs=(hbm,) * 3,
        scratch_shapes=[dma((3,))],
    )(*[pltpu.with_memory_space_constraint(result, pltpu.VMEM) for result in results])
    return layer_out[None], proj_grad[None], filter_grad


def solution(mesh):
    placed = (P("dp", None, None, "ctx"), P(), P(None, "ctx"), P(), P("dp", None, "ctx"))
    return jax.shard_map(
        shards,
        mesh=mesh,
        in_specs=placed,
        out_specs=(P("dp", None, "ctx"), P("dp", None, None, "ctx"), P("dp", "ctx")),
        check_vma=False,
    )
```

```python
import functools
import math

import jax
import jax.numpy as jnp
import ml_dtypes
import numpy as np
from jax import lax
from jax.experimental import pallas as pl
from jax.experimental.pallas import tpu as pltpu
from jax.sharding import PartitionSpec as P

DP = 4
CTX = 64
CHANNELS = 2048
LANES = 128
BLOCK = CHANNELS // DP
OWN = BLOCK // CTX
ROWS = OWN * CTX
POINTS = 2 * CTX * LANES
MESH = pl.DeviceIdType.MESH
F32 = jnp.float32
BF16 = jnp.bfloat16


def halves(table):
    high = table.astype(ml_dtypes.bfloat16)
    low = (table - high.astype(np.float64)).astype(ml_dtypes.bfloat16)
    return high, low


def tables():
    freq = np.arange(CTX) + 0.5
    block_angle = 2 * np.pi * np.outer(freq, np.arange(CTX)) / LANES
    first = np.concatenate([np.cos(block_angle), -np.sin(block_angle)], 0)
    first_hi, first_lo = halves(first)
    enter = np.concatenate([first_hi, first_lo], 1)
    last = np.concatenate([np.cos(block_angle.T), -np.sin(block_angle.T)], 1) * (2.0 / POINTS)
    last_hi, last_lo = halves(last)
    leave = np.concatenate([last_hi, last_lo], 1)
    inner = np.arange(LANES)
    inner_angle = 2 * np.pi * (np.outer(inner, inner) % LANES) / LANES
    c, s = np.cos(inner_angle), np.sin(inner_angle)
    spread_hi, spread_lo = halves(np.concatenate([np.concatenate([c, -s], 1), np.concatenate([s, c], 1)], 0))
    gather_hi, gather_lo = halves(np.concatenate([np.concatenate([c, s], 1), np.concatenate([-s, c], 1)], 0))
    twist = 2 * np.pi * np.outer(freq, inner) / POINTS
    turn = np.stack([np.cos(twist), np.sin(twist)]).astype(np.float32)
    widen = np.zeros((48, 10 * LANES), ml_dtypes.bfloat16)
    for part in range(3):
        for v in range(10):
            widen[16 * part + v, LANES * v : LANES * (v + 1)] = 1
    pick = np.zeros((2, 3, 8, LANES), ml_dtypes.bfloat16)
    place = np.zeros((2, 24, 3 * LANES), ml_dtypes.bfloat16)
    for m in range(3):
        for e in range(2):
            pick[0, m, 2 * m + e, LANES - 2 + e] = 1
            pick[1, m, 2 * m + e, e] = 1
            for part in range(3):
                place[0, 8 * part + 2 * m + e, LANES * m + e] = 1
                place[1, 8 * part + 2 * m + e, LANES * m + LANES - 2 + e] = 1
    return (enter, leave, spread_hi, spread_lo, gather_hi, gather_lo, turn, widen, pick, place)


def dot(a, b):
    return lax.dot_general(a, b, (((1,), (0,)), ((), ())), preferred_element_type=F32)


def dot_tn(a, b):
    return lax.dot_general(a, b, (((0,), (0,)), ((), ())), preferred_element_type=F32)


def dot_nt(a, b):
    return lax.dot_general(a, b, (((1,), (1,)), ((), ())), preferred_element_type=F32)


def split2(value):
    high = value.astype(BF16)
    return high, (value - high.astype(F32)).astype(BF16)


def split3(value):
    high = value.astype(BF16)
    rest = value - high.astype(F32)
    mid = rest.astype(BF16)
    return jnp.concatenate([high, mid, (rest - mid.astype(F32)).astype(BF16)], 0)


def loop(count, body, unroll=1):
    def step(i, carry):
        body(i)
        return carry

    lax.fori_loop(0, count, step, 0, unroll=unroll)


def kernel(
    proj_hbm, cot_hbm, filt_hbm, taps_hbm, gain_hbm, *refs,
):
    constants_hbm, refs = refs[:10], refs[10:]
    out_y, out_p, out_f = refs[:3]
    constants, refs = refs[3:13], refs[13:]
    enter, leave, spread_hi, spread_lo, gather_hi, gather_lo, turn, widen, pick, place = constants
    (
        proj, cot, filt, taps3, gains, taps,
        wide, acts, edge, sbuf, rbuf, csbuf, crbuf, fsend, frecv, fspec, total, work, zhi, zlo, spec, gsend, grecv,
        hx_send, hx_recv, hg_send, hg_recv,
        fwd_send, fwd_recv, back_send, back_recv, hg_ssem, hg_rsem, misc, in_sem, const_sem, ready,
    ) = refs
    d = lax.axis_index("dp")
    j = lax.axis_index("ctx")
    jy, jx, jz = j // 16, (j // 4) % 4, j % 4

    near = [((jx + n // 4) % 4) * 4 + (jz + n % 4) % 4 for n in range(16)]

    def others(i, act):
        def body(dy):
            plane = ((jy + dy) % 4) * 16
            pl.when(jnp.logical_or(dy > 0, i > 0))(lambda: act(plane + near[0]))
            for n in range(1, 16):
                act(plane + near[n])

        loop(4, body)

    def wait_bytes(ref, sem):
        pltpu.make_async_copy(ref, ref, sem).wait()

    rows_d = pl.ds(pl.multiple_of(d * BLOCK, BLOCK), BLOCK)
    loads = [
        pltpu.make_async_copy(source, target, in_sem.at[n])
        for n, (source, target) in enumerate((
            (proj_hbm, proj), (taps_hbm, taps3), (gain_hbm, gains), (filt_hbm.at[rows_d, :], filt), (cot_hbm, cot)))
    ]
    loads += [
        pltpu.make_async_copy(source, target, const_sem.at[n])
        for n, (source, target) in reversed(list(enumerate(zip(constants_hbm, constants))))
    ]
    for load in loads:
        load.start()

    @pl.when(j == 0)
    def _():
        hx_recv[...] = jnp.zeros_like(hx_recv)

    @pl.when(j == CTX - 1)
    def _():
        hg_recv[...] = jnp.zeros_like(hg_recv)

    barrier = pltpu.get_barrier_semaphore()

    others(0, lambda t: pl.semaphore_signal(barrier, inc=1, device_id=(d, t), device_id_type=MESH))
    for i in range(1, DP):
        pl.semaphore_signal(barrier, inc=1, device_id=((d + i) % DP, j), device_id_type=MESH)

    for load in loads[:3] + loads[5:8]:
        load.wait()
    taps[...] = jnp.zeros_like(taps)
    for m in range(3):
        taps[3 * m : 3 * m + 3, :] = taps3[m]
    taps[9:10, :] = gains[...]

    def prepare(b):
        cols = pl.ds(pl.multiple_of(b * BLOCK, BLOCK), BLOCK)
        picked = dot_nt(pick[0, 0], proj[0, cols, :])
        for m in range(1, 3):
            picked += dot_nt(pick[0, m], proj[m, cols, :])
        tap = taps[:, cols]
        rows = []
        for m in range(3):
            before, last = picked[2 * m : 2 * m + 1], picked[2 * m + 1 : 2 * m + 2]
            one, two = tap[3 * m + 1 : 3 * m + 2], tap[3 * m + 2 : 3 * m + 3]
            rows += [one * last + two * before, two * last]
        rows.append(jnp.zeros((2, BLOCK), F32))
        hx_send[b] = jnp.concatenate(rows, 0)

    loop(DP, prepare)
    loads[3].wait()

    def narrow(t):
        fsend[t] = filt[pl.ds(pl.multiple_of(t * OWN, OWN), OWN), :].astype(BF16)

    loop(CTX, narrow, unroll=8)
    pl.semaphore_wait(barrier, CTX - 1 + DP - 1)
    for i in range(1, DP):
        pl.semaphore_signal(ready, inc=1, device_id=((d + i) % DP, j), device_id_type=MESH)

    def halo_copy():
        return pltpu.make_async_remote_copy(
            src_ref=hx_send, dst_ref=hx_recv, send_sem=misc.at[0], recv_sem=misc.at[1],
            device_id=(d, jnp.minimum(j + 1, CTX - 1)), device_id_type=MESH)

    pl.when(j < CTX - 1)(lambda: halo_copy().start())

    def send_filter(t):
        pltpu.make_async_remote_copy(
            src_ref=fsend.at[t], dst_ref=frecv.at[j],
            send_sem=misc.at[2], recv_sem=misc.at[3], device_id=(d, t), device_id_type=MESH).start()

    others(0, send_filter)
    frecv[j] = fsend[j]
    loads[4].wait()

    def spread_taps(b):
        cols = pl.ds(pl.multiple_of(b * BLOCK, BLOCK), BLOCK)
        wide[cols, :] = dot_tn(split3(taps[:, cols]), widen[...])

    spread_taps(d)
    pl.when(j > 0)(lambda: wait_bytes(hx_recv, misc.at[1]))

    lane = lax.broadcasted_iota(jnp.int32, (2 * OWN, LANES), 1)

    def lanes_of(v):
        return slice(LANES * v, LANES * (v + 1))

    def gates(i):
        b = (d + i) % DP
        pl.when(i > 0)(lambda: spread_taps(b))
        edge[...] = dot_tn(split3(hx_recv[b]), place[0])

        def group(g):
            here = pl.ds(pl.multiple_of(g * 2 * OWN, 2 * OWN), 2 * OWN)
            rows = pl.ds(pl.multiple_of(b * BLOCK + g * 2 * OWN, 2 * OWN), 2 * OWN)
            act = []
            for m in range(3):
                x = proj[m, rows, :].astype(F32)
                one = jnp.where(lane >= 1, pltpu.roll(x, 1, 1), 0.0)
                two = jnp.where(lane >= 2, pltpu.roll(x, 2, 1), 0.0)
                value = (
                    wide[rows, lanes_of(3 * m)] * x
                    + wide[rows, lanes_of(3 * m + 1)] * one
                    + wide[rows, lanes_of(3 * m + 2)] * two
                    + edge[here, lanes_of(m)]
                )
                acts[m, rows, :] = value
                act.append(value)
            gate = act[0] * act[2]
            grad = cot[rows, :].astype(F32) * act[1]
            for e in range(2):
                part = slice(OWN * e, OWN * (e + 1))
                sbuf[i, 2 * g + e] = jnp.concatenate([gate[part], grad[part]], 0).astype(BF16)

        loop(CTX // 2, group, unroll=2)

        pl.when(i == 1)(lambda: pl.semaphore_wait(ready, DP - 1))

        def send(t):
            pltpu.make_async_remote_copy(
                src_ref=sbuf.at[i, t], dst_ref=rbuf.at[i, j], send_sem=fwd_send.at[i], recv_sem=fwd_recv.at[i],
                device_id=(b, t), device_id_type=MESH).start()

        others(i, send)

    loop(DP, gates)
    rbuf[0, j] = sbuf[0, j]

    def turned(real, imag, way):
        c, s = turn[0], turn[1]
        if way > 0:
            return real * c - imag * s, real * s + imag * c
        return real * c + imag * s, imag * c - real * s

    def put(rows, real, imag):
        for part, value in ((slice(0, LANES), real), (slice(LANES, 2 * LANES), imag)):
            high, low = split2(value)
            zhi[rows, part] = high
            zlo[rows, part] = low

    def across(count, table_hi, table_lo, into):
        def body(k):
            rows = pl.ds(pl.multiple_of(k * 512, 512), 512)
            into[rows, :] = (
                dot(zhi[rows, :], table_hi[...]) + dot(zlo[rows, :], table_hi[...]) + dot(zhi[rows, :], table_lo[...])
            )

        loop(count // 512, body)

    def rows_of(c):
        return pl.ds(pl.multiple_of(c * CTX, CTX), CTX)

    def enter_pair(product, row_left, row_right):
        for row, side in ((row_left, slice(0, LANES)), (row_right, slice(LANES, 2 * LANES))):
            put(rows_of(row), *turned(product[:CTX, side], product[CTX:, side], -1))

    def leave_pair(row_left, row_right):
        left = turned(spec[rows_of(row_left), :LANES], spec[rows_of(row_left), LANES:], 1)
        right = turned(spec[rows_of(row_right), :LANES], spec[rows_of(row_right), LANES:], 1)
        both = jnp.concatenate([jnp.concatenate([a, b], 1) for a, b in zip(left, right)], 0)
        high, low = split2(both)
        return dot(leave[...], jnp.concatenate([high, high], 0)) + dot(leave[:, :LANES], low)

    for load in loads[8:]:
        load.wait()
    wait_bytes(frecv.at[pl.ds(0, CTX - 1)], misc.at[3])

    def filter_unpack(p):
        work[pl.ds(pl.multiple_of(p * OWN, OWN), OWN), :] = frecv[p].astype(F32)

    loop(CTX, filter_unpack, unroll=8)

    def filter_enter(c):
        pair = jnp.concatenate(
            [work[pl.ds(c, CTX, stride=OWN), :], work[pl.ds(c + OWN // 2, CTX, stride=OWN), :]], 1
        ).astype(BF16)
        enter_pair(dot(enter[...], jnp.concatenate([pair, pair], 0)), c, c + OWN // 2)

    loop(OWN // 2, filter_enter)
    across(ROWS, spread_hi, spread_lo, fspec)
    total[...] = jnp.zeros_like(total)

    def convolve(i):
        @pl.when(i == 0)
        def _():
            wait_bytes(rbuf.at[0, pl.ds(0, CTX - 1)], fwd_recv.at[0])

        @pl.when(i > 0)
        def _():
            wait_bytes(rbuf.at[i], fwd_recv.at[i])

        def unpack(p):
            work[pl.ds(pl.multiple_of(p * 2 * OWN, 2 * OWN), 2 * OWN), :] = rbuf[i, p].astype(F32)

        loop(CTX, unpack, unroll=8)

        def one_enter(c):
            pair = jnp.concatenate(
                [work[pl.ds(c, CTX, stride=2 * OWN), :], work[pl.ds(c + OWN, CTX, stride=2 * OWN), :]], 1
            ).astype(BF16)
            enter_pair(dot(enter[...], jnp.concatenate([pair, pair], 0)), c, c + OWN)

        loop(OWN, one_enter, unroll=2)
        across(2 * ROWS, spread_hi, spread_lo, spec)

        def products(c):
            fr, fi = fspec[rows_of(c), :LANES], fspec[rows_of(c), LANES:]
            gr, gi = spec[rows_of(c), :LANES], spec[rows_of(c), LANES:]
            dr, di = spec[rows_of(c + OWN), :LANES], spec[rows_of(c + OWN), LANES:]
            put(rows_of(c), fr * gr - fi * gi, fr * gi + fi * gr)
            put(rows_of(c + OWN), fr * dr + fi * di, fr * di - fi * dr)
            total[rows_of(c), :LANES] += gr * dr + gi * di
            total[rows_of(c), LANES:] += gr * di - gi * dr

        loop(OWN, products)
        across(2 * ROWS, gather_hi, gather_lo, spec)

        def one_leave(c):
            result = leave_pair(c, c + OWN)
            work[pl.ds(c, CTX, stride=2 * OWN), :] = result[:, :LANES]
            work[pl.ds(c + OWN, CTX, stride=2 * OWN), :] = result[:, LANES:]

        loop(OWN, one_leave, unroll=2)

        def pack(p):
            csbuf[i, p] = work[pl.ds(pl.multiple_of(p * 2 * OWN, 2 * OWN), 2 * OWN), :].astype(BF16)

        loop(CTX, pack, unroll=8)
        home = (d + DP - i) % DP

        def send(t):
            pltpu.make_async_remote_copy(
                src_ref=csbuf.at[i, t], dst_ref=crbuf.at[i, j], send_sem=back_send.at[i], recv_sem=back_recv.at[i],
                device_id=(home, t), device_id_type=MESH).start()

        others(i, send)

    loop(DP, convolve)
    crbuf[0, j] = csbuf[0, j]

    def total_rows(c):
        put(rows_of(c), total[rows_of(c), :LANES], total[rows_of(c), LANES:])

    loop(OWN, total_rows)
    across(ROWS, gather_hi, gather_lo, spec)
    scale = 1.0 / math.sqrt(DP * CTX * LANES)

    def filter_leave(c):
        result = leave_pair(c, c + OWN // 2) * scale
        work[pl.ds(c, CTX, stride=OWN), :] = result[:, :LANES]
        work[pl.ds(c + OWN // 2, CTX, stride=OWN), :] = result[:, LANES:]

    loop(OWN // 2, filter_leave)

    def filter_pack(p):
        gsend[p] = work[pl.ds(pl.multiple_of(p * OWN, OWN), OWN), :].astype(BF16)

    loop(CTX, filter_pack, unroll=8)

    def send_grad(t):
        pltpu.make_async_remote_copy(
            src_ref=gsend.at[t], dst_ref=grecv.at[j],
            send_sem=misc.at[4], recv_sem=misc.at[5], device_id=(d, t), device_id_type=MESH).start()

    others(0, send_grad)
    grecv[j] = gsend[j]

    def grad_halo(i):
        b = (d + i) % DP
        return pltpu.make_async_remote_copy(
            src_ref=hg_send.at[b], dst_ref=hg_recv.at[b], send_sem=hg_ssem.at[i], recv_sem=hg_rsem.at[i],
            device_id=(d, jnp.maximum(j - 1, 0)), device_id_type=MESH)

    def outputs(i):
        b = (d + i) % DP

        @pl.when(i == 0)
        def _():
            wait_bytes(crbuf.at[0, pl.ds(0, CTX - 1)], back_recv.at[0])

        @pl.when(i > 0)
        def _():
            wait_bytes(crbuf.at[i], back_recv.at[i])

        def group(g):
            rows = pl.ds(pl.multiple_of(b * BLOCK + g * 2 * OWN, 2 * OWN), 2 * OWN)
            own = [sbuf[i, 2 * g + e].astype(F32) for e in range(2)]
            back = [crbuf[i, 2 * g + e].astype(F32) for e in range(2)]
            gate = jnp.concatenate([own[0][:OWN], own[1][:OWN]], 0)
            grad = jnp.concatenate([own[0][OWN:], own[1][OWN:]], 0)
            conv = jnp.concatenate([back[0][:OWN], back[1][:OWN]], 0)
            corr = jnp.concatenate([back[0][OWN:], back[1][OWN:]], 0)
            gain = wide[rows, lanes_of(9)]
            mixed = conv + gain * gate
            gate_grad = corr + gain * grad
            first, second, value = acts[0, rows, :], acts[1, rows, :], acts[2, rows, :]
            out_y[rows, :] = (second * mixed).astype(BF16)
            acts[0, rows, :] = gate_grad * value
            acts[1, rows, :] = cot[rows, :].astype(F32) * mixed
            acts[2, rows, :] = gate_grad * first

        loop(CTX // 2, group, unroll=2)
        cols = pl.ds(pl.multiple_of(b * BLOCK, BLOCK), BLOCK)
        picked = dot_nt(pick[1, 0], acts[0, cols, :].astype(BF16))
        for m in range(1, 3):
            picked += dot_nt(pick[1, m], acts[m, cols, :].astype(BF16))
        tap = taps[:, cols]
        rows = []
        for m in range(3):
            near, far = picked[2 * m : 2 * m + 1], picked[2 * m + 1 : 2 * m + 2]
            one, two = tap[3 * m + 1 : 3 * m + 2], tap[3 * m + 2 : 3 * m + 3]
            rows += [two * near, one * near + two * far]
        rows.append(jnp.zeros((2, BLOCK), F32))
        hg_send[b] = jnp.concatenate(rows, 0)
        pl.when(j > 0)(lambda: grad_halo(i).start())

    def finish(i):
        b = (d + i) % DP
        pl.when(j < CTX - 1)(lambda: grad_halo(i).wait_recv())
        edge[...] = dot_tn(split3(hg_recv[b]), place[1])

        def group(g):
            here = pl.ds(pl.multiple_of(g * 2 * OWN, 2 * OWN), 2 * OWN)
            rows = pl.ds(pl.multiple_of(b * BLOCK + g * 2 * OWN, 2 * OWN), 2 * OWN)
            for m in range(3):
                x = acts[m, rows, :]
                one = jnp.where(lane < LANES - 1, pltpu.roll(x, LANES - 1, 1), 0.0)
                two = jnp.where(lane < LANES - 2, pltpu.roll(x, LANES - 2, 1), 0.0)
                value = (
                    wide[rows, lanes_of(3 * m)] * x
                    + wide[rows, lanes_of(3 * m + 1)] * one
                    + wide[rows, lanes_of(3 * m + 2)] * two
                    + edge[here, lanes_of(m)]
                )
                out_p[m, rows, :] = value.astype(BF16)

        loop(CTX // 2, group, unroll=2)

    def tail(i):
        pl.when(i < DP)(lambda: outputs(i))
        pl.when(i > 0)(lambda: finish(i - 1))

    loop(DP + 1, tail)

    wait_bytes(grecv.at[pl.ds(0, CTX - 1)], misc.at[5])

    def filter_out(p):
        out_f[pl.ds(pl.multiple_of(p * OWN, OWN), OWN), :] = grecv[p].astype(F32)

    loop(CTX, filter_out, unroll=8)

    pl.when(j < CTX - 1)(lambda: halo_copy().wait_send())
    wait_bytes(fsend.at[pl.ds(0, CTX - 1)], misc.at[2])
    wait_bytes(gsend.at[pl.ds(0, CTX - 1)], misc.at[4])
    for i in range(DP):
        count = CTX - 1 if i == 0 else CTX
        wait_bytes(sbuf.at[i, pl.ds(0, count)], fwd_send.at[i])
        wait_bytes(csbuf.at[i, pl.ds(0, count)], back_send.at[i])
        pl.when(j > 0)(lambda i=i: grad_halo(i).wait_send())


def hand_over(*refs):
    count = len(refs) // 2
    sem = refs[-1]
    copies = [
        pltpu.make_async_copy(refs[n], refs[count + n], sem.at[n]) for n in range(count)
    ]
    for copy in copies:
        copy.start()
    for copy in copies:
        copy.wait()


def shards(projections, short_filter, long_filter, skip_gain, cotangent):
    constants = tables()
    near = pl.BlockSpec(memory_space=pltpu.VMEM)
    hbm = pl.BlockSpec(memory_space=pltpu.HBM)
    dma = pltpu.SemaphoreType.DMA
    vmem = pltpu.VMEM
    outs = (
        jax.ShapeDtypeStruct((CHANNELS, LANES), BF16),
        jax.ShapeDtypeStruct((3, CHANNELS, LANES), BF16),
        jax.ShapeDtypeStruct((ROWS, LANES), F32),
    )
    operands = (
        projections[0], cotangent[0], long_filter, short_filter.transpose(0, 2, 1), skip_gain[None], *constants
    )
    results = pl.pallas_call(
        kernel,
        out_shape=tuple(vmem(out.shape, out.dtype) for out in outs),
        in_specs=[hbm] * (5 + len(constants)),
        out_specs=(near,) * 3,
        scratch_shapes=[vmem(table.shape, jnp.dtype(table.dtype)) for table in constants]
        + [
            vmem((3, CHANNELS, LANES), BF16),
            vmem((CHANNELS, LANES), BF16),
            vmem((BLOCK, LANES), F32),
            vmem((3, 3, CHANNELS), F32),
            vmem((1, CHANNELS), F32),
            vmem((16, CHANNELS), F32),
            vmem((CHANNELS, 10 * LANES), F32),
            vmem((3, CHANNELS, LANES), F32),
            vmem((BLOCK, 3 * LANES), F32),
            vmem((DP, CTX, 2 * OWN, LANES), BF16),
            vmem((DP, CTX, 2 * OWN, LANES), BF16),
            vmem((DP, CTX, 2 * OWN, LANES), BF16),
            vmem((DP, CTX, 2 * OWN, LANES), BF16),
            vmem((CTX, OWN, LANES), BF16),
            vmem((CTX, OWN, LANES), BF16),
            vmem((ROWS, 2 * LANES), F32),
            vmem((ROWS, 2 * LANES), F32),
            vmem((2 * ROWS, LANES), F32),
            vmem((2 * ROWS, 2 * LANES), BF16),
            vmem((2 * ROWS, 2 * LANES), BF16),
            vmem((2 * ROWS, 2 * LANES), F32),
            vmem((CTX, OWN, LANES), BF16),
            vmem((CTX, OWN, LANES), BF16),
            vmem((DP, 8, BLOCK), F32),
            vmem((DP, 8, BLOCK), F32),
            vmem((DP, 8, BLOCK), F32),
            vmem((DP, 8, BLOCK), F32),
            dma((DP,)), dma((DP,)), dma((DP,)), dma((DP,)), dma((DP,)), dma((DP,)), dma((6,)),
            dma((5,)), dma((len(constants),)), pltpu.SemaphoreType.REGULAR,
        ],
        compiler_params=pltpu.CompilerParams(
            collective_id=0, has_side_effects=True, vmem_limit_bytes=48 * 1024 * 1024
        ),
    )(*[pltpu.with_memory_space_constraint(operand, pltpu.HBM) for operand in operands])
    layer_out, proj_grad, filter_grad = pl.pallas_call(
        hand_over,
        out_shape=outs,
        in_specs=[near] * 3,
        out_specs=(hbm,) * 3,
        scratch_shapes=[dma((3,))],
    )(*[pltpu.with_memory_space_constraint(result, pltpu.VMEM) for result in results])
    return layer_out[None], proj_grad[None], filter_grad


def solution(mesh):
    placed = (P("dp", None, None, "ctx"), P(), P(None, "ctx"), P(), P("dp", None, "ctx"))
    return jax.shard_map(
        shards,
        mesh=mesh,
        in_specs=placed,
        out_specs=(P("dp", None, "ctx"), P("dp", None, None, "ctx"), P("dp", "ctx")),
        check_vma=False,
    )
```

```python
import functools
import math

import jax
import jax.numpy as jnp
import ml_dtypes
import numpy as np
from jax import lax
from jax.experimental import pallas as pl
from jax.experimental.pallas import tpu as pltpu
from jax.sharding import PartitionSpec as P

DP = 4
CTX = 64
CHANNELS = 2048
LANES = 128
BLOCK = CHANNELS // DP
OWN = BLOCK // CTX
ROWS = OWN * CTX
POINTS = 2 * CTX * LANES
MESH = pl.DeviceIdType.MESH
F32 = jnp.float32
BF16 = jnp.bfloat16


def halves(table):
    high = table.astype(ml_dtypes.bfloat16)
    low = (table - high.astype(np.float64)).astype(ml_dtypes.bfloat16)
    return high, low


def tables():
    freq = np.arange(CTX) + 0.5
    block_angle = 2 * np.pi * np.outer(freq, np.arange(CTX)) / LANES
    first = np.concatenate([np.cos(block_angle), -np.sin(block_angle)], 0)
    first_hi, first_lo = halves(first)
    enter = np.concatenate([first_hi, first_lo], 1)
    last = np.concatenate([np.cos(block_angle.T), -np.sin(block_angle.T)], 1) * (2.0 / POINTS)
    last_hi, last_lo = halves(last)
    leave = np.concatenate([last_hi, last_lo], 1)
    inner = np.arange(LANES)
    inner_angle = 2 * np.pi * (np.outer(inner, inner) % LANES) / LANES
    c, s = np.cos(inner_angle), np.sin(inner_angle)
    spread_hi, spread_lo = halves(np.concatenate([np.concatenate([c, -s], 1), np.concatenate([s, c], 1)], 0))
    gather_hi, gather_lo = halves(np.concatenate([np.concatenate([c, s], 1), np.concatenate([-s, c], 1)], 0))
    twist = 2 * np.pi * np.outer(freq, inner) / POINTS
    turn = np.stack([np.cos(twist), np.sin(twist)]).astype(np.float32)
    widen = np.zeros((48, 10 * LANES), ml_dtypes.bfloat16)
    for part in range(3):
        for v in range(10):
            widen[16 * part + v, LANES * v : LANES * (v + 1)] = 1
    pick = np.zeros((2, 3, 8, LANES), ml_dtypes.bfloat16)
    place = np.zeros((2, 24, 3 * LANES), ml_dtypes.bfloat16)
    for m in range(3):
        for e in range(2):
            pick[0, m, 2 * m + e, LANES - 2 + e] = 1
            pick[1, m, 2 * m + e, e] = 1
            for part in range(3):
                place[0, 8 * part + 2 * m + e, LANES * m + e] = 1
                place[1, 8 * part + 2 * m + e, LANES * m + LANES - 2 + e] = 1
    return (enter, leave, spread_hi, spread_lo, gather_hi, gather_lo, turn, widen, pick, place)


def dot(a, b):
    return lax.dot_general(a, b, (((1,), (0,)), ((), ())), preferred_element_type=F32)


def dot_tn(a, b):
    return lax.dot_general(a, b, (((0,), (0,)), ((), ())), preferred_element_type=F32)


def dot_nt(a, b):
    return lax.dot_general(a, b, (((1,), (1,)), ((), ())), preferred_element_type=F32)


def split2(value):
    high = value.astype(BF16)
    return high, (value - high.astype(F32)).astype(BF16)


def split3(value):
    high = value.astype(BF16)
    rest = value - high.astype(F32)
    mid = rest.astype(BF16)
    return jnp.concatenate([high, mid, (rest - mid.astype(F32)).astype(BF16)], 0)


def loop(count, body, unroll=1):
    def step(i, carry):
        body(i)
        return carry

    lax.fori_loop(0, count, step, 0, unroll=unroll)


def kernel(
    proj_hbm, cot_hbm, filt_hbm, taps_hbm, gain_hbm, *refs,
):
    constants_hbm, refs = refs[:10], refs[10:]
    out_y, out_p, out_f = refs[:3]
    constants, refs = refs[3:13], refs[13:]
    enter, leave, spread_hi, spread_lo, gather_hi, gather_lo, turn, widen, pick, place = constants
    (
        proj, cot, filt, taps3, gains, taps,
        wide, acts, edge, sbuf, rbuf, csbuf, crbuf, fsend, frecv, fspec, total, work, zhi, zlo, spec, gsend, grecv,
        hx_send, hx_recv, hg_send, hg_recv,
        fwd_send, fwd_recv, back_send, back_recv, hg_ssem, hg_rsem, misc, in_sem, const_sem, ready,
    ) = refs
    d = lax.axis_index("dp")
    j = lax.axis_index("ctx")
    jy, jx, jz = j // 16, (j // 4) % 4, j % 4

    near = [((jx + n // 4) % 4) * 4 + (jz + n % 4) % 4 for n in range(16)]

    def others(i, act):
        def body(dy):
            plane = ((jy + dy) % 4) * 16
            pl.when(jnp.logical_or(dy > 0, i > 0))(lambda: act(plane + near[0]))
            for n in range(1, 16):
                act(plane + near[n])

        loop(4, body)

    def wait_bytes(ref, sem):
        pltpu.make_async_copy(ref, ref, sem).wait()

    rows_d = pl.ds(pl.multiple_of(d * BLOCK, BLOCK), BLOCK)
    loads = [
        pltpu.make_async_copy(source, target, in_sem.at[n])
        for n, (source, target) in enumerate((
            (proj_hbm, proj), (taps_hbm, taps3), (gain_hbm, gains), (filt_hbm.at[rows_d, :], filt), (cot_hbm, cot)))
    ]
    loads += [
        pltpu.make_async_copy(source, target, const_sem.at[n])
        for n, (source, target) in reversed(list(enumerate(zip(constants_hbm, constants))))
    ]
    for load in loads:
        load.start()

    @pl.when(j == 0)
    def _():
        hx_recv[...] = jnp.zeros_like(hx_recv)

    @pl.when(j == CTX - 1)
    def _():
        hg_recv[...] = jnp.zeros_like(hg_recv)

    barrier = pltpu.get_barrier_semaphore()

    others(0, lambda t: pl.semaphore_signal(barrier, inc=1, device_id=(d, t), device_id_type=MESH))
    for i in range(1, DP):
        pl.semaphore_signal(barrier, inc=1, device_id=((d + i) % DP, j), device_id_type=MESH)

    for load in loads[:3] + loads[5:8]:
        load.wait()
    taps[...] = jnp.zeros_like(taps)
    for m in range(3):
        taps[3 * m : 3 * m + 3, :] = taps3[m]
    taps[9:10, :] = gains[...]

    def prepare(b):
        cols = pl.ds(pl.multiple_of(b * BLOCK, BLOCK), BLOCK)
        picked = dot_nt(pick[0, 0], proj[0, cols, :])
        for m in range(1, 3):
            picked += dot_nt(pick[0, m], proj[m, cols, :])
        tap = taps[:, cols]
        rows = []
        for m in range(3):
            before, last = picked[2 * m : 2 * m + 1], picked[2 * m + 1 : 2 * m + 2]
            one, two = tap[3 * m + 1 : 3 * m + 2], tap[3 * m + 2 : 3 * m + 3]
            rows += [one * last + two * before, two * last]
        rows.append(jnp.zeros((2, BLOCK), F32))
        hx_send[b] = jnp.concatenate(rows, 0)

    loop(DP, prepare)
    loads[3].wait()

    def narrow(t):
        fsend[t] = filt[pl.ds(pl.multiple_of(t * OWN, OWN), OWN), :].astype(BF16)

    loop(CTX, narrow, unroll=8)
    pl.semaphore_wait(barrier, CTX - 1 + DP - 1)
    for i in range(1, DP):
        pl.semaphore_signal(ready, inc=1, device_id=((d + i) % DP, j), device_id_type=MESH)

    def halo_copy():
        return pltpu.make_async_remote_copy(
            src_ref=hx_send, dst_ref=hx_recv, send_sem=misc.at[0], recv_sem=misc.at[1],
            device_id=(d, jnp.minimum(j + 1, CTX - 1)), device_id_type=MESH)

    pl.when(j < CTX - 1)(lambda: halo_copy().start())

    def send_filter(t):
        pltpu.make_async_remote_copy(
            src_ref=fsend.at[t], dst_ref=frecv.at[j],
            send_sem=misc.at[2], recv_sem=misc.at[3], device_id=(d, t), device_id_type=MESH).start()

    others(0, send_filter)
    frecv[j] = fsend[j]
    loads[4].wait()

    def spread_taps(b):
        cols = pl.ds(pl.multiple_of(b * BLOCK, BLOCK), BLOCK)
        wide[cols, :] = dot_tn(split3(taps[:, cols]), widen[...])

    spread_taps(d)
    pl.when(j > 0)(lambda: wait_bytes(hx_recv, misc.at[1]))

    lane = lax.broadcasted_iota(jnp.int32, (2 * OWN, LANES), 1)

    def lanes_of(v):
        return slice(LANES * v, LANES * (v + 1))

    def gates(i):
        b = (d + i) % DP
        pl.when(i > 0)(lambda: spread_taps(b))
        edge[...] = dot_tn(split3(hx_recv[b]), place[0])

        pl.when(i == 1)(lambda: pl.semaphore_wait(ready, DP - 1))

        def group(pair):
            here = pl.ds(pl.multiple_of(pair * OWN, 2 * OWN), 2 * OWN)
            rows = pl.ds(pl.multiple_of(b * BLOCK + pair * OWN, 2 * OWN), 2 * OWN)
            act = []
            for m in range(3):
                x = proj[m, rows, :].astype(F32)
                one = jnp.where(lane >= 1, pltpu.roll(x, 1, 1), 0.0)
                two = jnp.where(lane >= 2, pltpu.roll(x, 2, 1), 0.0)
                value = (
                    wide[rows, lanes_of(3 * m)] * x
                    + wide[rows, lanes_of(3 * m + 1)] * one
                    + wide[rows, lanes_of(3 * m + 2)] * two
                    + edge[here, lanes_of(m)]
                )
                acts[m, rows, :] = value
                act.append(value)
            gate = act[0] * act[2]
            grad = cot[rows, :].astype(F32) * act[1]
            for e in range(2):
                part = slice(OWN * e, OWN * (e + 1))
                sbuf[i, pair + e] = jnp.concatenate([gate[part], grad[part]], 0).astype(BF16)

        def send(t):
            pltpu.make_async_remote_copy(
                src_ref=sbuf.at[i, t], dst_ref=rbuf.at[i, j], send_sem=fwd_send.at[i], recv_sem=fwd_recv.at[i],
                device_id=(b, t), device_id_type=MESH).start()

        def quarter(dy):
            plane = ((jy + dy) % 4) * 16
            pairs = [plane + ((jx + n // 2) % 4) * 4 + ((jz // 2 + n % 2) % 2) * 2 for n in range(8)]
            for pair in pairs:
                group(pair)
            for n, pair in enumerate(pairs):
                for e in range(2):
                    t = pair + e
                    if n == 0:
                        pl.when(jnp.logical_or(i > 0, t != j))(lambda t=t: send(t))
                    else:
                        send(t)

        loop(4, quarter)

    loop(DP, gates)
    rbuf[0, j] = sbuf[0, j]

    def turned(real, imag, way):
        c, s = turn[0], turn[1]
        if way > 0:
            return real * c - imag * s, real * s + imag * c
        return real * c + imag * s, imag * c - real * s

    def put(rows, real, imag):
        for part, value in ((slice(0, LANES), real), (slice(LANES, 2 * LANES), imag)):
            high, low = split2(value)
            zhi[rows, part] = high
            zlo[rows, part] = low

    def across(count, table_hi, table_lo, into):
        def body(k):
            rows = pl.ds(pl.multiple_of(k * 512, 512), 512)
            into[rows, :] = (
                dot(zhi[rows, :], table_hi[...]) + dot(zlo[rows, :], table_hi[...]) + dot(zhi[rows, :], table_lo[...])
            )

        loop(count // 512, body)

    def rows_of(c):
        return pl.ds(pl.multiple_of(c * CTX, CTX), CTX)

    def enter_pair(product, row_left, row_right):
        for row, side in ((row_left, slice(0, LANES)), (row_right, slice(LANES, 2 * LANES))):
            put(rows_of(row), *turned(product[:CTX, side], product[CTX:, side], -1))

    def leave_pair(row_left, row_right):
        left = turned(spec[rows_of(row_left), :LANES], spec[rows_of(row_left), LANES:], 1)
        right = turned(spec[rows_of(row_right), :LANES], spec[rows_of(row_right), LANES:], 1)
        both = jnp.concatenate([jnp.concatenate([a, b], 1) for a, b in zip(left, right)], 0)
        high, low = split2(both)
        return dot(leave[...], jnp.concatenate([high, high], 0)) + dot(leave[:, :LANES], low)

    for load in loads[8:]:
        load.wait()
    wait_bytes(frecv.at[pl.ds(0, CTX - 1)], misc.at[3])

    def filter_unpack(p):
        work[pl.ds(pl.multiple_of(p * OWN, OWN), OWN), :] = frecv[p].astype(F32)

    loop(CTX, filter_unpack, unroll=8)

    def filter_enter(c):
        pair = jnp.concatenate(
            [work[pl.ds(c, CTX, stride=OWN), :], work[pl.ds(c + OWN // 2, CTX, stride=OWN), :]], 1
        ).astype(BF16)
        enter_pair(dot(enter[...], jnp.concatenate([pair, pair], 0)), c, c + OWN // 2)

    loop(OWN // 2, filter_enter)
    across(ROWS, spread_hi, spread_lo, fspec)
    total[...] = jnp.zeros_like(total)

    def convolve(i):
        @pl.when(i == 0)
        def _():
            wait_bytes(rbuf.at[0, pl.ds(0, CTX - 1)], fwd_recv.at[0])

        @pl.when(i > 0)
        def _():
            wait_bytes(rbuf.at[i], fwd_recv.at[i])

        def unpack(p):
            work[pl.ds(pl.multiple_of(p * 2 * OWN, 2 * OWN), 2 * OWN), :] = rbuf[i, p].astype(F32)

        loop(CTX, unpack, unroll=8)

        def one_enter(c):
            pair = jnp.concatenate(
                [work[pl.ds(c, CTX, stride=2 * OWN), :], work[pl.ds(c + OWN, CTX, stride=2 * OWN), :]], 1
            ).astype(BF16)
            enter_pair(dot(enter[...], jnp.concatenate([pair, pair], 0)), c, c + OWN)

        loop(OWN, one_enter, unroll=2)
        across(2 * ROWS, spread_hi, spread_lo, spec)

        def products(c):
            fr, fi = fspec[rows_of(c), :LANES], fspec[rows_of(c), LANES:]
            gr, gi = spec[rows_of(c), :LANES], spec[rows_of(c), LANES:]
            dr, di = spec[rows_of(c + OWN), :LANES], spec[rows_of(c + OWN), LANES:]
            put(rows_of(c), fr * gr - fi * gi, fr * gi + fi * gr)
            put(rows_of(c + OWN), fr * dr + fi * di, fr * di - fi * dr)
            total[rows_of(c), :LANES] += gr * dr + gi * di
            total[rows_of(c), LANES:] += gr * di - gi * dr

        loop(OWN, products)
        across(2 * ROWS, gather_hi, gather_lo, spec)

        def one_leave(c):
            result = leave_pair(c, c + OWN)
            work[pl.ds(c, CTX, stride=2 * OWN), :] = result[:, :LANES]
            work[pl.ds(c + OWN, CTX, stride=2 * OWN), :] = result[:, LANES:]

        loop(OWN, one_leave, unroll=2)

        def pack(p):
            csbuf[i, p] = work[pl.ds(pl.multiple_of(p * 2 * OWN, 2 * OWN), 2 * OWN), :].astype(BF16)

        loop(CTX, pack, unroll=8)
        home = (d + DP - i) % DP

        def send(t):
            pltpu.make_async_remote_copy(
                src_ref=csbuf.at[i, t], dst_ref=crbuf.at[i, j], send_sem=back_send.at[i], recv_sem=back_recv.at[i],
                device_id=(home, t), device_id_type=MESH).start()

        others(i, send)

    loop(DP, convolve)
    crbuf[0, j] = csbuf[0, j]

    def total_rows(c):
        put(rows_of(c), total[rows_of(c), :LANES], total[rows_of(c), LANES:])

    loop(OWN, total_rows)
    across(ROWS, gather_hi, gather_lo, spec)
    scale = 1.0 / math.sqrt(DP * CTX * LANES)

    def filter_leave(c):
        result = leave_pair(c, c + OWN // 2) * scale
        work[pl.ds(c, CTX, stride=OWN), :] = result[:, :LANES]
        work[pl.ds(c + OWN // 2, CTX, stride=OWN), :] = result[:, LANES:]

    loop(OWN // 2, filter_leave)

    def filter_pack(p):
        gsend[p] = work[pl.ds(pl.multiple_of(p * OWN, OWN), OWN), :].astype(BF16)

    loop(CTX, filter_pack, unroll=8)

    def send_grad(t):
        pltpu.make_async_remote_copy(
            src_ref=gsend.at[t], dst_ref=grecv.at[j],
            send_sem=misc.at[4], recv_sem=misc.at[5], device_id=(d, t), device_id_type=MESH).start()

    others(0, send_grad)
    grecv[j] = gsend[j]

    def grad_halo(i):
        b = (d + i) % DP
        return pltpu.make_async_remote_copy(
            src_ref=hg_send.at[b], dst_ref=hg_recv.at[b], send_sem=hg_ssem.at[i], recv_sem=hg_rsem.at[i],
            device_id=(d, jnp.maximum(j - 1, 0)), device_id_type=MESH)

    def outputs(i):
        b = (d + i) % DP

        @pl.when(i == 0)
        def _():
            wait_bytes(crbuf.at[0, pl.ds(0, CTX - 1)], back_recv.at[0])

        @pl.when(i > 0)
        def _():
            wait_bytes(crbuf.at[i], back_recv.at[i])

        def group(g):
            rows = pl.ds(pl.multiple_of(b * BLOCK + g * 2 * OWN, 2 * OWN), 2 * OWN)
            own = [sbuf[i, 2 * g + e].astype(F32) for e in range(2)]
            back = [crbuf[i, 2 * g + e].astype(F32) for e in range(2)]
            gate = jnp.concatenate([own[0][:OWN], own[1][:OWN]], 0)
            grad = jnp.concatenate([own[0][OWN:], own[1][OWN:]], 0)
            conv = jnp.concatenate([back[0][:OWN], back[1][:OWN]], 0)
            corr = jnp.concatenate([back[0][OWN:], back[1][OWN:]], 0)
            gain = wide[rows, lanes_of(9)]
            mixed = conv + gain * gate
            gate_grad = corr + gain * grad
            first, second, value = acts[0, rows, :], acts[1, rows, :], acts[2, rows, :]
            out_y[rows, :] = (second * mixed).astype(BF16)
            acts[0, rows, :] = gate_grad * value
            acts[1, rows, :] = cot[rows, :].astype(F32) * mixed
            acts[2, rows, :] = gate_grad * first

        loop(CTX // 2, group, unroll=8)
        cols = pl.ds(pl.multiple_of(b * BLOCK, BLOCK), BLOCK)
        picked = dot_nt(pick[1, 0], acts[0, cols, :].astype(BF16))
        for m in range(1, 3):
            picked += dot_nt(pick[1, m], acts[m, cols, :].astype(BF16))
        tap = taps[:, cols]
        rows = []
        for m in range(3):
            near, far = picked[2 * m : 2 * m + 1], picked[2 * m + 1 : 2 * m + 2]
            one, two = tap[3 * m + 1 : 3 * m + 2], tap[3 * m + 2 : 3 * m + 3]
            rows += [two * near, one * near + two * far]
        rows.append(jnp.zeros((2, BLOCK), F32))
        hg_send[b] = jnp.concatenate(rows, 0)
        pl.when(j > 0)(lambda: grad_halo(i).start())

    def finish(i):
        b = (d + i) % DP
        pl.when(j < CTX - 1)(lambda: grad_halo(i).wait_recv())
        edge[...] = dot_tn(split3(hg_recv[b]), place[1])

        def group(g):
            here = pl.ds(pl.multiple_of(g * 2 * OWN, 2 * OWN), 2 * OWN)
            rows = pl.ds(pl.multiple_of(b * BLOCK + g * 2 * OWN, 2 * OWN), 2 * OWN)
            for m in range(3):
                x = acts[m, rows, :]
                one = jnp.where(lane < LANES - 1, pltpu.roll(x, LANES - 1, 1), 0.0)
                two = jnp.where(lane < LANES - 2, pltpu.roll(x, LANES - 2, 1), 0.0)
                value = (
                    wide[rows, lanes_of(3 * m)] * x
                    + wide[rows, lanes_of(3 * m + 1)] * one
                    + wide[rows, lanes_of(3 * m + 2)] * two
                    + edge[here, lanes_of(m)]
                )
                out_p[m, rows, :] = value.astype(BF16)

        loop(CTX // 2, group, unroll=8)

    def tail(i):
        pl.when(i < DP)(lambda: outputs(i))
        pl.when(i > 0)(lambda: finish(i - 1))

    loop(DP + 1, tail)

    wait_bytes(grecv.at[pl.ds(0, CTX - 1)], misc.at[5])

    def filter_out(p):
        out_f[pl.ds(pl.multiple_of(p * OWN, OWN), OWN), :] = grecv[p].astype(F32)

    loop(CTX, filter_out, unroll=8)

    pl.when(j < CTX - 1)(lambda: halo_copy().wait_send())
    wait_bytes(fsend.at[pl.ds(0, CTX - 1)], misc.at[2])
    wait_bytes(gsend.at[pl.ds(0, CTX - 1)], misc.at[4])
    for i in range(DP):
        count = CTX - 1 if i == 0 else CTX
        wait_bytes(sbuf.at[i, pl.ds(0, count)], fwd_send.at[i])
        wait_bytes(csbuf.at[i, pl.ds(0, count)], back_send.at[i])
        pl.when(j > 0)(lambda i=i: grad_halo(i).wait_send())


def hand_over(*refs):
    count = len(refs) // 2
    sem = refs[-1]
    copies = [
        pltpu.make_async_copy(refs[n], refs[count + n], sem.at[n]) for n in range(count)
    ]
    for copy in copies:
        copy.start()
    for copy in copies:
        copy.wait()


def shards(projections, short_filter, long_filter, skip_gain, cotangent):
    constants = tables()
    near = pl.BlockSpec(memory_space=pltpu.VMEM)
    hbm = pl.BlockSpec(memory_space=pltpu.HBM)
    dma = pltpu.SemaphoreType.DMA
    vmem = pltpu.VMEM
    outs = (
        jax.ShapeDtypeStruct((CHANNELS, LANES), BF16),
        jax.ShapeDtypeStruct((3, CHANNELS, LANES), BF16),
        jax.ShapeDtypeStruct((ROWS, LANES), F32),
    )
    operands = (
        projections[0], cotangent[0], long_filter, short_filter.transpose(0, 2, 1), skip_gain[None], *constants
    )
    results = pl.pallas_call(
        kernel,
        out_shape=tuple(vmem(out.shape, out.dtype) for out in outs),
        in_specs=[hbm] * (5 + len(constants)),
        out_specs=(near,) * 3,
        scratch_shapes=[vmem(table.shape, jnp.dtype(table.dtype)) for table in constants]
        + [
            vmem((3, CHANNELS, LANES), BF16),
            vmem((CHANNELS, LANES), BF16),
            vmem((BLOCK, LANES), F32),
            vmem((3, 3, CHANNELS), F32),
            vmem((1, CHANNELS), F32),
            vmem((16, CHANNELS), F32),
            vmem((CHANNELS, 10 * LANES), F32),
            vmem((3, CHANNELS, LANES), F32),
            vmem((BLOCK, 3 * LANES), F32),
            vmem((DP, CTX, 2 * OWN, LANES), BF16),
            vmem((DP, CTX, 2 * OWN, LANES), BF16),
            vmem((DP, CTX, 2 * OWN, LANES), BF16),
            vmem((DP, CTX, 2 * OWN, LANES), BF16),
            vmem((CTX, OWN, LANES), BF16),
            vmem((CTX, OWN, LANES), BF16),
            vmem((ROWS, 2 * LANES), F32),
            vmem((ROWS, 2 * LANES), F32),
            vmem((2 * ROWS, LANES), F32),
            vmem((2 * ROWS, 2 * LANES), BF16),
            vmem((2 * ROWS, 2 * LANES), BF16),
            vmem((2 * ROWS, 2 * LANES), F32),
            vmem((CTX, OWN, LANES), BF16),
            vmem((CTX, OWN, LANES), BF16),
            vmem((DP, 8, BLOCK), F32),
            vmem((DP, 8, BLOCK), F32),
            vmem((DP, 8, BLOCK), F32),
            vmem((DP, 8, BLOCK), F32),
            dma((DP,)), dma((DP,)), dma((DP,)), dma((DP,)), dma((DP,)), dma((DP,)), dma((6,)),
            dma((5,)), dma((len(constants),)), pltpu.SemaphoreType.REGULAR,
        ],
        compiler_params=pltpu.CompilerParams(
            collective_id=0, has_side_effects=True, vmem_limit_bytes=48 * 1024 * 1024
        ),
    )(*[pltpu.with_memory_space_constraint(operand, pltpu.HBM) for operand in operands])
    layer_out, proj_grad, filter_grad = pl.pallas_call(
        hand_over,
        out_shape=outs,
        in_specs=[near] * 3,
        out_specs=(hbm,) * 3,
        scratch_shapes=[dma((3,))],
    )(*[pltpu.with_memory_space_constraint(result, pltpu.VMEM) for result in results])
    return layer_out[None], proj_grad[None], filter_grad


def solution(mesh):
    placed = (P("dp", None, None, "ctx"), P(), P(None, "ctx"), P(), P("dp", None, "ctx"))
    return jax.shard_map(
        shards,
        mesh=mesh,
        in_specs=placed,
        out_specs=(P("dp", None, "ctx"), P("dp", None, None, "ctx"), P("dp", "ctx")),
        check_vma=False,
    )
```

```python
import functools
import math

import jax
import jax.numpy as jnp
import ml_dtypes
import numpy as np
from jax import lax
from jax.experimental import pallas as pl
from jax.experimental.pallas import tpu as pltpu
from jax.sharding import PartitionSpec as P

DP = 4
CTX = 64
CHANNELS = 2048
LANES = 128
BLOCK = CHANNELS // DP
OWN = BLOCK // CTX
ROWS = OWN * CTX
POINTS = 2 * CTX * LANES
MESH = pl.DeviceIdType.MESH
F32 = jnp.float32
BF16 = jnp.bfloat16


def halves(table):
    high = table.astype(ml_dtypes.bfloat16)
    low = (table - high.astype(np.float64)).astype(ml_dtypes.bfloat16)
    return high, low


def tables():
    freq = np.arange(CTX) + 0.5
    block_angle = 2 * np.pi * np.outer(freq, np.arange(CTX)) / LANES
    first = np.concatenate([np.cos(block_angle), -np.sin(block_angle)], 0)
    first_hi, first_lo = halves(first)
    enter = np.concatenate([first_hi, first_lo], 1)
    last = np.concatenate([np.cos(block_angle.T), -np.sin(block_angle.T)], 1) * (2.0 / POINTS)
    last_hi, last_lo = halves(last)
    leave = np.concatenate([last_hi, last_lo], 1)
    inner = np.arange(LANES)
    inner_angle = 2 * np.pi * (np.outer(inner, inner) % LANES) / LANES
    c, s = np.cos(inner_angle), np.sin(inner_angle)
    spread_hi, spread_lo = halves(np.concatenate([np.concatenate([c, -s], 1), np.concatenate([s, c], 1)], 0))
    gather_hi, gather_lo = halves(np.concatenate([np.concatenate([c, s], 1), np.concatenate([-s, c], 1)], 0))
    twist = 2 * np.pi * np.outer(freq, inner) / POINTS
    turn = np.stack([np.cos(twist), np.sin(twist)]).astype(np.float32)
    widen = np.zeros((48, 10 * LANES), ml_dtypes.bfloat16)
    for part in range(3):
        for v in range(10):
            widen[16 * part + v, LANES * v : LANES * (v + 1)] = 1
    pick = np.zeros((2, 3, 8, LANES), ml_dtypes.bfloat16)
    place = np.zeros((2, 24, 3 * LANES), ml_dtypes.bfloat16)
    for m in range(3):
        for e in range(2):
            pick[0, m, 2 * m + e, LANES - 2 + e] = 1
            pick[1, m, 2 * m + e, e] = 1
            for part in range(3):
                place[0, 8 * part + 2 * m + e, LANES * m + e] = 1
                place[1, 8 * part + 2 * m + e, LANES * m + LANES - 2 + e] = 1
    return (enter, leave, spread_hi, spread_lo, gather_hi, gather_lo, turn, widen, pick, place)


def dot(a, b):
    return lax.dot_general(a, b, (((1,), (0,)), ((), ())), preferred_element_type=F32)


def dot_tn(a, b):
    return lax.dot_general(a, b, (((0,), (0,)), ((), ())), preferred_element_type=F32)


def dot_nt(a, b):
    return lax.dot_general(a, b, (((1,), (1,)), ((), ())), preferred_element_type=F32)


def split2(value):
    high = value.astype(BF16)
    return high, (value - high.astype(F32)).astype(BF16)


def split3(value):
    high = value.astype(BF16)
    rest = value - high.astype(F32)
    mid = rest.astype(BF16)
    return jnp.concatenate([high, mid, (rest - mid.astype(F32)).astype(BF16)], 0)


def loop(count, body, unroll=1):
    def step(i, carry):
        body(i)
        return carry

    lax.fori_loop(0, count, step, 0, unroll=unroll)


def kernel(
    proj_hbm, cot_hbm, filt_hbm, taps_hbm, gain_hbm, *refs,
):
    constants_hbm, refs = refs[:10], refs[10:]
    out_y, out_p, out_f = refs[:3]
    constants, refs = refs[3:13], refs[13:]
    enter, leave, spread_hi, spread_lo, gather_hi, gather_lo, turn, widen, pick, place = constants
    (
        proj, cot, filt, taps3, gains, taps,
        wide, acts, edge, sbuf, rbuf, csbuf, crbuf, fsend, frecv, fspec, total, work, zhi, zlo, spec, gsend, grecv,
        hx_send, hx_recv, hg_send, hg_recv,
        fwd_send, fwd_recv, back_send, back_recv, hg_ssem, hg_rsem, misc, in_sem, const_sem, ready,
    ) = refs
    d = lax.axis_index("dp")
    j = lax.axis_index("ctx")
    jy, jx, jz = j // 16, (j // 4) % 4, j % 4

    near = [((jx + n // 4) % 4) * 4 + (jz + n % 4) % 4 for n in range(16)]

    def others(i, act):
        def body(dy):
            plane = ((jy + dy) % 4) * 16
            pl.when(jnp.logical_or(dy > 0, i > 0))(lambda: act(plane + near[0]))
            for n in range(1, 16):
                act(plane + near[n])

        loop(4, body)

    def wait_bytes(ref, sem):
        pltpu.make_async_copy(ref, ref, sem).wait()

    rows_d = pl.ds(pl.multiple_of(d * BLOCK, BLOCK), BLOCK)
    loads = [
        pltpu.make_async_copy(source, target, in_sem.at[n])
        for n, (source, target) in enumerate((
            (proj_hbm, proj), (taps_hbm, taps3), (gain_hbm, gains), (filt_hbm.at[rows_d, :], filt), (cot_hbm, cot)))
    ]
    loads += [
        pltpu.make_async_copy(source, target, const_sem.at[n])
        for n, (source, target) in reversed(list(enumerate(zip(constants_hbm, constants))))
    ]
    for load in loads:
        load.start()

    @pl.when(j == 0)
    def _():
        hx_recv[...] = jnp.zeros_like(hx_recv)

    @pl.when(j == CTX - 1)
    def _():
        hg_recv[...] = jnp.zeros_like(hg_recv)

    barrier = pltpu.get_barrier_semaphore()

    others(0, lambda t: pl.semaphore_signal(barrier, inc=1, device_id=(d, t), device_id_type=MESH))
    for i in range(1, DP):
        pl.semaphore_signal(barrier, inc=1, device_id=((d + i) % DP, j), device_id_type=MESH)

    for load in loads[:3] + loads[5:8]:
        load.wait()
    taps[...] = jnp.zeros_like(taps)
    for m in range(3):
        taps[3 * m : 3 * m + 3, :] = taps3[m]
    taps[9:10, :] = gains[...]

    def prepare(b):
        cols = pl.ds(pl.multiple_of(b * BLOCK, BLOCK), BLOCK)
        picked = dot_nt(pick[0, 0], proj[0, cols, :])
        for m in range(1, 3):
            picked += dot_nt(pick[0, m], proj[m, cols, :])
        tap = taps[:, cols]
        rows = []
        for m in range(3):
            before, last = picked[2 * m : 2 * m + 1], picked[2 * m + 1 : 2 * m + 2]
            one, two = tap[3 * m + 1 : 3 * m + 2], tap[3 * m + 2 : 3 * m + 3]
            rows += [one * last + two * before, two * last]
        rows.append(jnp.zeros((2, BLOCK), F32))
        hx_send[b] = jnp.concatenate(rows, 0)

    loop(DP, prepare)
    loads[3].wait()

    def narrow(t):
        fsend[t] = filt[pl.ds(pl.multiple_of(t * OWN, OWN), OWN), :].astype(BF16)

    loop(CTX, narrow, unroll=8)
    def spread_taps(b):
        cols = pl.ds(pl.multiple_of(b * BLOCK, BLOCK), BLOCK)
        wide[cols, :] = dot_tn(split3(taps[:, cols]), widen[...])

    spread_taps(d)
    pl.semaphore_wait(barrier, CTX - 1 + DP - 1)
    for i in range(1, DP):
        pl.semaphore_signal(ready, inc=1, device_id=((d + i) % DP, j), device_id_type=MESH)

    def halo_copy():
        return pltpu.make_async_remote_copy(
            src_ref=hx_send, dst_ref=hx_recv, send_sem=misc.at[0], recv_sem=misc.at[1],
            device_id=(d, jnp.minimum(j + 1, CTX - 1)), device_id_type=MESH)

    pl.when(j < CTX - 1)(lambda: halo_copy().start())

    def send_filter(t):
        pltpu.make_async_remote_copy(
            src_ref=fsend.at[t], dst_ref=frecv.at[j],
            send_sem=misc.at[2], recv_sem=misc.at[3], device_id=(d, t), device_id_type=MESH).start()

    others(0, send_filter)
    frecv[j] = fsend[j]
    loads[4].wait()

    pl.when(j > 0)(lambda: wait_bytes(hx_recv, misc.at[1]))

    lane = lax.broadcasted_iota(jnp.int32, (2 * OWN, LANES), 1)

    def lanes_of(v):
        return slice(LANES * v, LANES * (v + 1))

    def gates(i):
        b = (d + i) % DP
        pl.when(i > 0)(lambda: spread_taps(b))
        edge[...] = dot_tn(split3(hx_recv[b]), place[0])

        pl.when(i == 1)(lambda: pl.semaphore_wait(ready, DP - 1))

        def group(pair):
            here = pl.ds(pl.multiple_of(pair * OWN, 2 * OWN), 2 * OWN)
            rows = pl.ds(pl.multiple_of(b * BLOCK + pair * OWN, 2 * OWN), 2 * OWN)
            act = []
            for m in range(3):
                x = proj[m, rows, :].astype(F32)
                one = jnp.where(lane >= 1, pltpu.roll(x, 1, 1), 0.0)
                two = jnp.where(lane >= 2, pltpu.roll(x, 2, 1), 0.0)
                value = (
                    wide[rows, lanes_of(3 * m)] * x
                    + wide[rows, lanes_of(3 * m + 1)] * one
                    + wide[rows, lanes_of(3 * m + 2)] * two
                    + edge[here, lanes_of(m)]
                )
                acts[m, rows, :] = value
                act.append(value)
            gate = act[0] * act[2]
            grad = cot[rows, :].astype(F32) * act[1]
            for e in range(2):
                part = slice(OWN * e, OWN * (e + 1))
                sbuf[i, pair + e] = jnp.concatenate([gate[part], grad[part]], 0).astype(BF16)

        def send(t):
            pltpu.make_async_remote_copy(
                src_ref=sbuf.at[i, t], dst_ref=rbuf.at[i, j], send_sem=fwd_send.at[i], recv_sem=fwd_recv.at[i],
                device_id=(b, t), device_id_type=MESH).start()

        def quarter(dy):
            plane = ((jy + dy) % 4) * 16
            pairs = [plane + ((jx + n // 2) % 4) * 4 + ((jz // 2 + n % 2) % 2) * 2 for n in range(8)]
            for pair in pairs:
                group(pair)
            for n, pair in enumerate(pairs):
                for e in range(2):
                    t = pair + e
                    if n == 0:
                        pl.when(jnp.logical_or(i > 0, t != j))(lambda t=t: send(t))
                    else:
                        send(t)

        loop(4, quarter)

    loop(DP, gates)
    rbuf[0, j] = sbuf[0, j]

    def turned(real, imag, way):
        c, s = turn[0], turn[1]
        if way > 0:
            return real * c - imag * s, real * s + imag * c
        return real * c + imag * s, imag * c - real * s

    def put(rows, real, imag):
        for part, value in ((slice(0, LANES), real), (slice(LANES, 2 * LANES), imag)):
            high, low = split2(value)
            zhi[rows, part] = high
            zlo[rows, part] = low

    def across(count, table_hi, table_lo, into):
        def body(k):
            rows = pl.ds(pl.multiple_of(k * 512, 512), 512)
            into[rows, :] = (
                dot(zhi[rows, :], table_hi[...]) + dot(zlo[rows, :], table_hi[...]) + dot(zhi[rows, :], table_lo[...])
            )

        loop(count // 512, body)

    def rows_of(c):
        return pl.ds(pl.multiple_of(c * CTX, CTX), CTX)

    def enter_pair(product, row_left, row_right):
        for row, side in ((row_left, slice(0, LANES)), (row_right, slice(LANES, 2 * LANES))):
            put(rows_of(row), *turned(product[:CTX, side], product[CTX:, side], -1))

    def leave_pair(row_left, row_right):
        left = turned(spec[rows_of(row_left), :LANES], spec[rows_of(row_left), LANES:], 1)
        right = turned(spec[rows_of(row_right), :LANES], spec[rows_of(row_right), LANES:], 1)
        both = jnp.concatenate([jnp.concatenate([a, b], 1) for a, b in zip(left, right)], 0)
        high, low = split2(both)
        return dot(leave[...], jnp.concatenate([high, high], 0)) + dot(leave[:, :LANES], low)

    for load in loads[8:]:
        load.wait()
    wait_bytes(frecv.at[pl.ds(0, CTX - 1)], misc.at[3])

    def filter_unpack(p):
        work[pl.ds(pl.multiple_of(p * OWN, OWN), OWN), :] = frecv[p].astype(F32)

    loop(CTX, filter_unpack, unroll=8)

    def filter_enter(c):
        pair = jnp.concatenate(
            [work[pl.ds(c, CTX, stride=OWN), :], work[pl.ds(c + OWN // 2, CTX, stride=OWN), :]], 1
        ).astype(BF16)
        enter_pair(dot(enter[...], jnp.concatenate([pair, pair], 0)), c, c + OWN // 2)

    loop(OWN // 2, filter_enter)
    across(ROWS, spread_hi, spread_lo, fspec)
    total[...] = jnp.zeros_like(total)

    def convolve(i):
        @pl.when(i == 0)
        def _():
            wait_bytes(rbuf.at[0, pl.ds(0, CTX - 1)], fwd_recv.at[0])

        @pl.when(i > 0)
        def _():
            wait_bytes(rbuf.at[i], fwd_recv.at[i])

        def unpack(p):
            work[pl.ds(pl.multiple_of(p * 2 * OWN, 2 * OWN), 2 * OWN), :] = rbuf[i, p].astype(F32)

        loop(CTX, unpack, unroll=8)

        def one_enter(c):
            pair = jnp.concatenate(
                [work[pl.ds(c, CTX, stride=2 * OWN), :], work[pl.ds(c + OWN, CTX, stride=2 * OWN), :]], 1
            ).astype(BF16)
            enter_pair(dot(enter[...], jnp.concatenate([pair, pair], 0)), c, c + OWN)

        loop(OWN, one_enter, unroll=2)
        across(2 * ROWS, spread_hi, spread_lo, spec)

        def products(c):
            fr, fi = fspec[rows_of(c), :LANES], fspec[rows_of(c), LANES:]
            gr, gi = spec[rows_of(c), :LANES], spec[rows_of(c), LANES:]
            dr, di = spec[rows_of(c + OWN), :LANES], spec[rows_of(c + OWN), LANES:]
            put(rows_of(c), fr * gr - fi * gi, fr * gi + fi * gr)
            put(rows_of(c + OWN), fr * dr + fi * di, fr * di - fi * dr)
            total[rows_of(c), :LANES] += gr * dr + gi * di
            total[rows_of(c), LANES:] += gr * di - gi * dr

        loop(OWN, products)
        across(2 * ROWS, gather_hi, gather_lo, spec)

        def one_leave(c):
            result = leave_pair(c, c + OWN)
            work[pl.ds(c, CTX, stride=2 * OWN), :] = result[:, :LANES]
            work[pl.ds(c + OWN, CTX, stride=2 * OWN), :] = result[:, LANES:]

        loop(OWN, one_leave, unroll=2)

        def pack(p):
            csbuf[i, p] = work[pl.ds(pl.multiple_of(p * 2 * OWN, 2 * OWN), 2 * OWN), :].astype(BF16)

        loop(CTX, pack, unroll=8)
        home = (d + DP - i) % DP

        def send(t):
            pltpu.make_async_remote_copy(
                src_ref=csbuf.at[i, t], dst_ref=crbuf.at[i, j], send_sem=back_send.at[i], recv_sem=back_recv.at[i],
                device_id=(home, t), device_id_type=MESH).start()

        others(i, send)

    loop(DP, convolve)
    crbuf[0, j] = csbuf[0, j]

    def total_rows(c):
        put(rows_of(c), total[rows_of(c), :LANES], total[rows_of(c), LANES:])

    loop(OWN, total_rows)
    across(ROWS, gather_hi, gather_lo, spec)
    scale = 1.0 / math.sqrt(DP * CTX * LANES)

    def filter_leave(c):
        result = leave_pair(c, c + OWN // 2) * scale
        work[pl.ds(c, CTX, stride=OWN), :] = result[:, :LANES]
        work[pl.ds(c + OWN // 2, CTX, stride=OWN), :] = result[:, LANES:]

    loop(OWN // 2, filter_leave)

    def filter_pack(p):
        gsend[p] = work[pl.ds(pl.multiple_of(p * OWN, OWN), OWN), :].astype(BF16)

    loop(CTX, filter_pack, unroll=8)

    def send_grad(t):
        pltpu.make_async_remote_copy(
            src_ref=gsend.at[t], dst_ref=grecv.at[j],
            send_sem=misc.at[4], recv_sem=misc.at[5], device_id=(d, t), device_id_type=MESH).start()

    grecv[j] = gsend[j]

    def grad_halo(i):
        b = (d + i) % DP
        return pltpu.make_async_remote_copy(
            src_ref=hg_send.at[b], dst_ref=hg_recv.at[b], send_sem=hg_ssem.at[i], recv_sem=hg_rsem.at[i],
            device_id=(d, jnp.maximum(j - 1, 0)), device_id_type=MESH)

    def outputs(i):
        b = (d + i) % DP

        @pl.when(i == 0)
        def _():
            wait_bytes(crbuf.at[0, pl.ds(0, CTX - 1)], back_recv.at[0])

        @pl.when(i > 0)
        def _():
            wait_bytes(crbuf.at[i], back_recv.at[i])

        def group(g):
            rows = pl.ds(pl.multiple_of(b * BLOCK + g * 2 * OWN, 2 * OWN), 2 * OWN)
            own = [sbuf[i, 2 * g + e].astype(F32) for e in range(2)]
            back = [crbuf[i, 2 * g + e].astype(F32) for e in range(2)]
            gate = jnp.concatenate([own[0][:OWN], own[1][:OWN]], 0)
            grad = jnp.concatenate([own[0][OWN:], own[1][OWN:]], 0)
            conv = jnp.concatenate([back[0][:OWN], back[1][:OWN]], 0)
            corr = jnp.concatenate([back[0][OWN:], back[1][OWN:]], 0)
            gain = wide[rows, lanes_of(9)]
            mixed = conv + gain * gate
            gate_grad = corr + gain * grad
            first, second, value = acts[0, rows, :], acts[1, rows, :], acts[2, rows, :]
            out_y[rows, :] = (second * mixed).astype(BF16)
            acts[0, rows, :] = gate_grad * value
            acts[1, rows, :] = cot[rows, :].astype(F32) * mixed
            acts[2, rows, :] = gate_grad * first

        loop(CTX // 2, group, unroll=8)
        cols = pl.ds(pl.multiple_of(b * BLOCK, BLOCK), BLOCK)
        picked = dot_nt(pick[1, 0], acts[0, cols, :].astype(BF16))
        for m in range(1, 3):
            picked += dot_nt(pick[1, m], acts[m, cols, :].astype(BF16))
        tap = taps[:, cols]
        rows = []
        for m in range(3):
            near, far = picked[2 * m : 2 * m + 1], picked[2 * m + 1 : 2 * m + 2]
            one, two = tap[3 * m + 1 : 3 * m + 2], tap[3 * m + 2 : 3 * m + 3]
            rows += [two * near, one * near + two * far]
        rows.append(jnp.zeros((2, BLOCK), F32))
        hg_send[b] = jnp.concatenate(rows, 0)
        pl.when(j > 0)(lambda: grad_halo(i).start())

    def finish(i):
        b = (d + i) % DP
        pl.when(j < CTX - 1)(lambda: grad_halo(i).wait_recv())
        edge[...] = dot_tn(split3(hg_recv[b]), place[1])

        def group(g):
            here = pl.ds(pl.multiple_of(g * 2 * OWN, 2 * OWN), 2 * OWN)
            rows = pl.ds(pl.multiple_of(b * BLOCK + g * 2 * OWN, 2 * OWN), 2 * OWN)
            for m in range(3):
                x = acts[m, rows, :]
                one = jnp.where(lane < LANES - 1, pltpu.roll(x, LANES - 1, 1), 0.0)
                two = jnp.where(lane < LANES - 2, pltpu.roll(x, LANES - 2, 1), 0.0)
                value = (
                    wide[rows, lanes_of(3 * m)] * x
                    + wide[rows, lanes_of(3 * m + 1)] * one
                    + wide[rows, lanes_of(3 * m + 2)] * two
                    + edge[here, lanes_of(m)]
                )
                out_p[m, rows, :] = value.astype(BF16)

        loop(CTX // 2, group, unroll=8)

    def tail(i):
        pl.when(i < DP)(lambda: outputs(i))
        pl.when(i == DP - 2)(lambda: others(0, send_grad))
        pl.when(i > 0)(lambda: finish(i - 1))

    loop(DP + 1, tail)

    wait_bytes(grecv.at[pl.ds(0, CTX - 1)], misc.at[5])

    def filter_out(p):
        out_f[pl.ds(pl.multiple_of(p * OWN, OWN), OWN), :] = grecv[p].astype(F32)

    loop(CTX, filter_out, unroll=8)

    pl.when(j < CTX - 1)(lambda: halo_copy().wait_send())
    wait_bytes(fsend.at[pl.ds(0, CTX - 1)], misc.at[2])
    wait_bytes(gsend.at[pl.ds(0, CTX - 1)], misc.at[4])
    for i in range(DP):
        count = CTX - 1 if i == 0 else CTX
        wait_bytes(sbuf.at[i, pl.ds(0, count)], fwd_send.at[i])
        wait_bytes(csbuf.at[i, pl.ds(0, count)], back_send.at[i])
        pl.when(j > 0)(lambda i=i: grad_halo(i).wait_send())


def hand_over(*refs):
    count = len(refs) // 2
    sem = refs[-1]
    copies = [
        pltpu.make_async_copy(refs[n], refs[count + n], sem.at[n]) for n in range(count)
    ]
    for copy in copies:
        copy.start()
    for copy in copies:
        copy.wait()


def shards(projections, short_filter, long_filter, skip_gain, cotangent):
    constants = tables()
    near = pl.BlockSpec(memory_space=pltpu.VMEM)
    hbm = pl.BlockSpec(memory_space=pltpu.HBM)
    dma = pltpu.SemaphoreType.DMA
    vmem = pltpu.VMEM
    outs = (
        jax.ShapeDtypeStruct((CHANNELS, LANES), BF16),
        jax.ShapeDtypeStruct((3, CHANNELS, LANES), BF16),
        jax.ShapeDtypeStruct((ROWS, LANES), F32),
    )
    operands = (
        projections[0], cotangent[0], long_filter, short_filter.transpose(0, 2, 1), skip_gain[None], *constants
    )
    results = pl.pallas_call(
        kernel,
        out_shape=tuple(vmem(out.shape, out.dtype) for out in outs),
        in_specs=[hbm] * (5 + len(constants)),
        out_specs=(near,) * 3,
        scratch_shapes=[vmem(table.shape, jnp.dtype(table.dtype)) for table in constants]
        + [
            vmem((3, CHANNELS, LANES), BF16),
            vmem((CHANNELS, LANES), BF16),
            vmem((BLOCK, LANES), F32),
            vmem((3, 3, CHANNELS), F32),
            vmem((1, CHANNELS), F32),
            vmem((16, CHANNELS), F32),
            vmem((CHANNELS, 10 * LANES), F32),
            vmem((3, CHANNELS, LANES), F32),
            vmem((BLOCK, 3 * LANES), F32),
            vmem((DP, CTX, 2 * OWN, LANES), BF16),
            vmem((DP, CTX, 2 * OWN, LANES), BF16),
            vmem((DP, CTX, 2 * OWN, LANES), BF16),
            vmem((DP, CTX, 2 * OWN, LANES), BF16),
            vmem((CTX, OWN, LANES), BF16),
            vmem((CTX, OWN, LANES), BF16),
            vmem((ROWS, 2 * LANES), F32),
            vmem((ROWS, 2 * LANES), F32),
            vmem((2 * ROWS, LANES), F32),
            vmem((2 * ROWS, 2 * LANES), BF16),
            vmem((2 * ROWS, 2 * LANES), BF16),
            vmem((2 * ROWS, 2 * LANES), F32),
            vmem((CTX, OWN, LANES), BF16),
            vmem((CTX, OWN, LANES), BF16),
            vmem((DP, 8, BLOCK), F32),
            vmem((DP, 8, BLOCK), F32),
            vmem((DP, 8, BLOCK), F32),
            vmem((DP, 8, BLOCK), F32),
            dma((DP,)), dma((DP,)), dma((DP,)), dma((DP,)), dma((DP,)), dma((DP,)), dma((6,)),
            dma((5,)), dma((len(constants),)), pltpu.SemaphoreType.REGULAR,
        ],
        compiler_params=pltpu.CompilerParams(
            collective_id=0, has_side_effects=True, vmem_limit_bytes=48 * 1024 * 1024
        ),
    )(*[pltpu.with_memory_space_constraint(operand, pltpu.HBM) for operand in operands])
    layer_out, proj_grad, filter_grad = pl.pallas_call(
        hand_over,
        out_shape=outs,
        in_specs=[near] * 3,
        out_specs=(hbm,) * 3,
        scratch_shapes=[dma((3,))],
    )(*[pltpu.with_memory_space_constraint(result, pltpu.VMEM) for result in results])
    return layer_out[None], proj_grad[None], filter_grad


def solution(mesh):
    placed = (P("dp", None, None, "ctx"), P(), P(None, "ctx"), P(), P("dp", None, "ctx"))
    return jax.shard_map(
        shards,
        mesh=mesh,
        in_specs=placed,
        out_specs=(P("dp", None, "ctx"), P("dp", None, None, "ctx"), P("dp", "ctx")),
        check_vma=False,
    )
```
